512 devices in a mesh: xt: 32 (over z, x), yt: 16 (over y, core).
Axes of the slice: x: 4, y: 8, z: 8, core: 2. Of those that a mesh axis runs over, the one named last changes fastest.
Arguments:
- pressure: float32 [8, 256, 2048], P(None, 'xt', 'yt'), may hold values from -1 to 1
- saturation: float32 [2, 8, 256, 2048], P(None, None, 'xt', 'yt'), may hold values from 0.05 to 0.45
- old_mass: float32 [3, 8, 256, 2048], P(None, None, 'xt', 'yt'), may hold values from 0.05 to 0.5
- pore_volume: float32 [8, 256, 2048], P(None, 'xt', 'yt'), may hold values from 0.2 to 2
- transmissibility: float32 [3, 8, 256, 2048], P(None, None, 'xt', 'yt'), may hold values from 1 to 10
- upwind_code: int32 [8, 256, 2048], P(None, 'xt', 'yt'), may hold values from 0 to 511
- cell_tangent: float32 [2, 3, 8, 256, 2048], P(None, None, None, 'xt', 'yt'), may hold values from -6 to 6
- segment_pressure: float32 [128, 4096], P('yt', 'xt'), may hold values from -1 to 1
- segment_tangent: float32 [2, 128, 4096], P(None, 'yt', 'xt'), may hold values from -6 to 6
- segment_well: int32 [128, 4096], P('yt', 'xt'), may hold values from 0 to 255, never falling along the last dimension, each value on 1 to 32 neighbouring positions
- link_factor: float32 [128, 4096], P('yt', 'xt'), may hold values from 0.5 to 5
- heel_pressure: float32 [128, 4096], P('yt', 'xt'), may hold values from -2 to 0
- perforation_cell: int32 [16, 16384], P('yt', 'xt'), may hold values from 0 to 8191
- perforation_segment: int32 [16, 16384], P('yt', 'xt'), may hold values from 0 to 1023
- well_index: float32 [16, 16384], P('yt', 'xt'), may hold values from 1 to 10
- perforation_count: int32 [16, 1024], P('yt', 'xt'), may hold values from 0 to 16, as said below
Outputs:
- residual: float32 [3, 8, 256, 2048], P(None, None, 'xt', 'yt')
- cell_products: float32 [2, 3, 8, 256, 2048], P(None, None, None, 'xt', 'yt')
- segment_residual: float32 [3, 128, 4096], P(None, 'yt', 'xt')
The draws below stay inside these ranges and needn't reach their ends.
Inputs may be any that keep to these rules, and one draw needn't show every extreme that they name: `upwind_code`: bit 3 * d + a set: phase a on the face after the cell along direction d takes the mobility of the next cell. `perforation_cell`: local number of a cell of the slot's own device. `perforation_segment`: slot k * 16 + m names a segment of the device with xt index k and the same yt index, by its number r * 128 + c in that device's block. `perforation_count`: entry k of a device: how many of its slots toward xt index k are live (the first ones). For each yt index some xt index gets 16 from every device of that yt index. `segment_well`: never falls along a row; a run of equal numbers is one well.
All inputs are finite; a program needn't handle non-finite values.
Results may differ from the reference program's by a relative error of at most 0.0003.
Values sent between devices are 32-bit elements; how exact they have to be, the bound alone decides.
No kernel may reach another device: no remote copies, remote signals or barrier semaphores. Data moves between devices by JAX's collectives and lax.ppermute only.
A program may use at most 128 MiB of HBM per device.

```python
import math
import jax
import jax.numpy as jnp
import numpy as np
from jax import lax

NZ = 8
CX = 8
CY = 128
SEG_Y = 8
SEG_DEV = 128
PEER_MOST = 16
NX = 256
NY = 2048
NSY = 128
NSX = 4096
N_XT = 32
N_YT = 16


def draw_perforation_count(key, part):
    key = jax.random.fold_in(key, 11)
    key_base, key_star = jax.random.split(key)
    base_counts = jax.random.randint(key_base, (N_YT, N_XT * N_XT), 0, PEER_MOST + 1)
    star_tile = jax.random.randint(key_star, (N_YT, 1), 0, N_XT)
    target_tile = jnp.arange(N_XT * N_XT, dtype=jnp.int32).reshape(1, N_XT * N_XT) % N_XT
    return jnp.where(target_tile == star_tile, PEER_MOST, base_counts).astype(jnp.int32)


def set_ends(values, key, smallest, top_value):
    shape = values.shape
    spot = [jax.random.randint(jax.random.fold_in(key, axis), (), 0, shape[axis]) for axis in range(len(shape))]
    values = values.at[tuple(spot)].set(smallest)
    longest = shape.index(max(shape))
    spot[longest] = (spot[longest] + 1) % shape[longest]
    return values.at[tuple(spot)].set(top_value)


def shard_levels(key, shape, shards, least, top_value):
    def one(dim, parts):
        steps = jax.random.uniform(jax.random.fold_in(jax.random.fold_in(key, 6), dim), (parts,), jnp.float32, least / len(shards), top_value / len(shards))
        return jnp.repeat(jnp.exp(steps), shape[dim] // parts).reshape((-1,) + (1,) * (len(shape) - dim - 1))

    loudness = one(*shards[0])
    for cut in shards[1:]:
        loudness = loudness * one(*cut)
    return loudness


def profile(count, total, most, skew):
    portions = [(1 << 20) // math.isqrt(rank ** skew) + 1 for rank in range(2, count + 1)]
    spare, holding = total - most - (count - 1), [1] * (count - 1)
    while spare > 0:
        movable = [i for i in range(count - 1) if holding[i] < most]
        whole, left = sum([portions[i] for i in movable]), spare
        for i in movable:
            addition = min(most - holding[i], max(1, left * portions[i] // whole), spare)
            holding[i] = holding[i] + addition
            spare = spare - addition
    return np.array([most] + holding)


def ragged(own_key, count, total, limit, slope):
    if count == 2:
        one = jax.random.randint(own_key, (), max(1, total - limit), min(limit, total - 1) + 1)
        return jnp.stack([one, total - one])
    tallies = jnp.asarray(profile(count, total, limit, slope), jnp.int32)
    twos = (count - 1) // 2
    giver, sink = tallies[1:1 + 2 * twos:2], tallies[2:2 + 2 * twos:2]
    margin = jnp.minimum(giver - 1, limit - sink)
    shifted = jax.random.randint(jax.random.fold_in(own_key, 1), (twos,), 0, 1 << 20) % (margin + 1)
    tallies = tallies.at[1:1 + 2 * twos:2].set(giver - shifted).at[2:2 + 2 * twos:2].set(sink + shifted)
    return tallies[jax.random.permutation(jax.random.fold_in(own_key, 2), count)]


def gaussian(stream_key, shape, spread, most, cuts=(), kind=jnp.bfloat16):
    values = jax.random.normal(stream_key, shape, jnp.float32) * spread
    if len(cuts) > 0:
        values = shard_levels(stream_key, shape, cuts, -0.22, 0.18) * values
    return jnp.clip(values, min=-most, max=most).astype(kind)


def setup_inputs(seed: int = 0) -> dict:
    key_list = jax.random.split(jax.random.key(seed), 17)
    return {
        "pressure": jnp.clip(jax.random.uniform(key_list[0], (NZ, NX, NY), jnp.float32, -1.0, 1.0) * shard_levels(key_list[0], (NZ, NX, NY), ((1, 32), (2, 16)), -0.4, 0.0), -1.0, 1.0),
        "saturation": jnp.clip(0.05 + 0.39999999 * jax.random.uniform(key_list[1], (2, NZ, NX, NY), jnp.float32) ** shard_levels(key_list[1], (2, NZ, NX, NY), ((2, 32), (3, 16)), -0.2, 0.2), 0.05, 0.45),
        "old_mass": jnp.clip(0.05 + 0.45 * jax.random.uniform(key_list[2], (3, NZ, NX, NY), jnp.float32) ** shard_levels(key_list[2], (3, NZ, NX, NY), ((2, 32), (3, 16)), -0.2, 0.2), 0.05, 0.5),
        "pore_volume": jnp.clip(jnp.exp(math.log(2.0) - 2.3025851 * jax.random.uniform(key_list[3], (NZ, NX, NY), jnp.float32) ** shard_levels(key_list[3], (NZ, NX, NY), ((1, 32), (2, 16)), -0.2, 0.2)), 0.2, 2.0),
        "transmissibility": jnp.clip(jnp.exp(math.log(10.0) - 2.3025851 * jax.random.uniform(key_list[4], (3, NZ, NX, NY), jnp.float32) ** shard_levels(key_list[4], (3, NZ, NX, NY), ((2, 32), (3, 16)), -0.2, 0.2)), 1.0, 10.0),
        "upwind_code": set_ends(jax.random.randint(key_list[5], (NZ, NX, NY), 0, 512), jax.random.fold_in(key_list[5], 1), 0, 511).astype(jnp.int32),
        "cell_tangent": gaussian(key_list[6], (2, 3, NZ, NX, NY), 1.0, 6.0, ((3, 32), (4, 16)), jnp.float32),
        "segment_pressure": jnp.clip(jax.random.uniform(key_list[7], (NSY, NSX), jnp.float32, -1.0, 1.0) * shard_levels(key_list[7], (NSY, NSX), ((0, 16), (1, 32)), -0.4, 0.0), -1.0, 1.0),
        "segment_tangent": gaussian(key_list[8], (2, NSY, NSX), 1.0, 6.0, ((1, 16), (2, 32)), jnp.float32),
        "segment_well": jax.vmap(lambda own: jnp.searchsorted(jnp.cumsum(ragged(own, SEG_DEV * N_XT // 16, NSX, min(32, SEG_DEV * N_XT // 2), 1)), jnp.arange(NSX), side="right"))(jax.random.split(key_list[9], NSY)).reshape((NSY, NSX)).astype(jnp.int32),
        "link_factor": jnp.clip(jnp.exp(math.log(5.0) - 2.3025851 * jax.random.uniform(key_list[10], (NSY, NSX), jnp.float32) ** shard_levels(key_list[10], (NSY, NSX), ((0, 16), (1, 32)), -0.2, 0.2)), 0.5, 5.0),
        "heel_pressure": jnp.clip(-2.0 + 2.0 * jax.random.uniform(key_list[11], (NSY, NSX), jnp.float32) ** shard_levels(key_list[11], (NSY, NSX), ((0, 16), (1, 32)), -0.2, 0.2), -2.0, 0.0),
        "perforation_cell": set_ends(jax.random.randint(key_list[12], (N_YT, N_XT * N_XT * PEER_MOST), 0, NZ * CX * CY), jax.random.fold_in(key_list[12], 1), 0, (NZ * CX * CY) - 1).astype(jnp.int32),
        "perforation_segment": set_ends(jax.random.randint(key_list[13], (N_YT, N_XT * N_XT * PEER_MOST), 0, SEG_Y * SEG_DEV), jax.random.fold_in(key_list[13], 1), 0, (SEG_Y * SEG_DEV) - 1).astype(jnp.int32),
        "well_index": jnp.clip(jnp.exp(math.log(10.0) - 2.3025851 * jax.random.uniform(key_list[14], (N_YT, N_XT * N_XT * PEER_MOST), jnp.float32) ** shard_levels(key_list[14], (N_YT, N_XT * N_XT * PEER_MOST), ((0, 16), (1, 32)), -0.2, 0.2)), 1.0, 10.0),
        "perforation_count": draw_perforation_count(jax.random.fold_in(key_list[16], 71), 0),
    }


COMPRESS = (0.05, 0.1, 0.6)
VISCOSITY = (0.5, 2.0, 0.2)
GRAVITY_HEAD = (0.3, 0.25, 0.05)


def properties(pressure, water, gas):
    oil = 1.0 - water - gas
    mobility_list = []
    mass_list = []
    for phase, phase_saturation in enumerate((water, oil, gas)):
        density = jnp.exp(COMPRESS[phase] * pressure)
        phase_mass = density * phase_saturation
        mobility_list.append(phase_mass * phase_saturation / VISCOSITY[phase])
        mass_list.append(phase_mass)
    return jnp.stack(mobility_list), jnp.stack(mass_list)


def phase_bits(code_array, direction):
    return jnp.stack([(code_array // (2 ** (3 * direction + phase))) % 2 for phase in range(3)])


def cut(array_in, start, stop, axis_at):
    return lax.slice_in_dim(array_in, start, stop, axis=axis_at)


def cell_terms(pressure, saturation, segment_pressure, old_mass, pore_volume, transmissibility, upwind_code,
               segment_well, link_factor, heel_pressure, perforation_cell, perforation_segment, well_index,
               perforation_count):
    mobility, mass = properties(pressure, saturation[0], saturation[1])
    cell_balance = pore_volume * mass - old_mass
    for direction, spatial in ((0, 1), (1, 2), (2, 0)):
        extent = pressure.shape[spatial]
        mob_lower = cut(mobility, 0, extent - 1, spatial + 1)
        mob_upper = cut(mobility, 1, extent, spatial + 1)
        press_diff = cut(pressure, 0, extent - 1, spatial) - cut(pressure, 1, extent, spatial)
        upwind_bits = phase_bits(cut(upwind_code, 0, extent - 1, spatial), direction)
        upwind_mob = jnp.where(upwind_bits == 1, mob_upper, mob_lower)
        head_values = GRAVITY_HEAD if direction == 2 else (0.0, 0.0, 0.0)
        gravity_head = jnp.asarray(head_values, dtype=jnp.float32).reshape(3, 1, 1, 1)
        face_flux = cut(transmissibility[direction], 0, extent - 1, spatial) * upwind_mob * (press_diff[None] + gravity_head)
        widths_after = [(0, 0)] * 4
        widths_after[spatial + 1] = (0, 1)
        widths_before = [(0, 0)] * 4
        widths_before[spatial + 1] = (1, 0)
        cell_balance = cell_balance + jnp.pad(face_flux, widths_after) - jnp.pad(face_flux, widths_before)
    tile_y = jnp.arange(N_YT, dtype=jnp.int32).reshape(N_YT, 1, 1, 1)
    tile_x = jnp.arange(N_XT, dtype=jnp.int32).reshape(1, N_XT, 1, 1)
    owner_tile = jnp.arange(N_XT, dtype=jnp.int32).reshape(1, 1, N_XT, 1)
    slot_rank = jnp.arange(PEER_MOST, dtype=jnp.int32).reshape(1, 1, 1, PEER_MOST)
    slot_shape = (N_YT, N_XT, N_XT, PEER_MOST)
    slot_cells = perforation_cell.reshape(slot_shape)
    layer_of = slot_cells // (CX * CY)
    global_x = tile_x * CX + (slot_cells // CY) % CX
    global_y = tile_y * CY + slot_cells % CY
    slot_segments = perforation_segment.reshape(slot_shape)
    segment_rowid = tile_y * SEG_Y + slot_segments // SEG_DEV
    segment_col = owner_tile * SEG_DEV + slot_segments % SEG_DEV
    live_slot = slot_rank < perforation_count.reshape(N_YT, N_XT, N_XT, 1)
    weight = jnp.where(live_slot, well_index.reshape(slot_shape), 0.0)
    pressure_drop = pressure[layer_of, global_x, global_y] - segment_pressure[segment_rowid, segment_col]
    rates = weight * mobility[:, layer_of, global_x, global_y] * pressure_drop
    cell_balance = cell_balance.at[:, layer_of, global_x, global_y].add(rates)
    inflow = jnp.zeros_like(segment_pressure).at[segment_rowid, segment_col].add(rates.sum(0))
    next_press = jnp.concatenate([segment_pressure[:, 1:], jnp.zeros_like(segment_pressure[:, :1])], 1)
    next_well = jnp.concatenate([segment_well[:, 1:], jnp.full_like(segment_well[:, :1], -1)], 1)
    linked = next_well == segment_well
    link_flow = link_factor * (segment_pressure - jnp.where(linked, next_press, heel_pressure))
    carried = jnp.where(linked, link_flow, 0.0)
    segment_balance = inflow - link_flow + jnp.pad(carried[:, :-1], ((0, 0), (1, 0)))
    return cell_balance, segment_balance


def reference(pressure, saturation, old_mass, pore_volume, transmissibility, upwind_code, cell_tangent,
              segment_pressure, segment_tangent, segment_well, link_factor, heel_pressure, perforation_cell,
              perforation_segment, well_index, perforation_count):
    def evaluate(press_in, sat_in, seg_in):
        return cell_terms(press_in, sat_in, seg_in, old_mass, pore_volume, transmissibility, upwind_code,
                          segment_well, link_factor, heel_pressure, perforation_cell, perforation_segment,
                          well_index, perforation_count)

    primals = (pressure, saturation, segment_pressure)
    (residual, segment_value), (cell_first, segment_first) = jax.jvp(
        evaluate, primals, (cell_tangent[0, 0], cell_tangent[0, 1:], segment_tangent[0]))
    ignored, (cell_second, segment_second) = jax.jvp(
        evaluate, primals, (cell_tangent[1, 0], cell_tangent[1, 1:], segment_tangent[1]))
    return (residual, jnp.stack([cell_first, cell_second]),
            jnp.stack([segment_value, segment_first, segment_second]))
```

```python
import jax
import jax.numpy as jnp
from jax import lax
from jax.experimental import pallas as pl
from jax.experimental.pallas import tpu as pltpu
from jax.sharding import PartitionSpec as P

COMPRESS = (0.05, 0.1, 0.6)
INV_VISCOSITY = (2.0, 0.5, 5.0)
GRAVITY_HEAD = (0.3, 0.25, 0.05)

NZ = 8
LANES = 128
CELL_ROWS = 64
SLOTS = 512
TILES = 32
PEER = 16
ROWS_A = 24
F32 = jnp.float32
BF16 = jnp.bfloat16
VMEM = pl.BlockSpec(memory_space=pltpu.VMEM)


def roll(x, shift, axis):
    return pltpu.roll(x, shift % x.shape[axis], axis)


def iota(shape, dim):
    return lax.broadcasted_iota(jnp.int32, shape, dim)


def split(x):
    hi = x.astype(BF16)
    lo = (x - hi.astype(F32)).astype(BF16)
    return hi, lo


def one_hot(mask):
    return jnp.where(mask, 1.0, 0.0).astype(BF16)


def properties(press, water, gas):
    oil = (1.0 - water[0] - gas[0], -water[1] - gas[1], -water[2] - gas[2])
    mobility, mass = [], []
    for phase, sat in enumerate((water, oil, gas)):
        c = COMPRESS[phase]
        base = jnp.exp(c * press[0])
        cb = c * base
        m0 = base * sat[0]
        cs = cb * sat[0]
        m1 = cs * press[1] + base * sat[1]
        m2 = cs * press[2] + base * sat[2]
        v = INV_VISCOSITY[phase]
        vs = v * sat[0]
        vm = v * m0
        mobility.append((m0 * vs, m1 * vs + vm * sat[1], m2 * vs + vm * sat[2]))
        mass.append((m0, m1, m2))
    return mobility, mass


def fluxes(mob_low, mob_up, press_low, press_up, trans, code, direction, heads):
    drop = [trans * (press_low[s] - press_up[s]) for s in range(3)]
    out = []
    for phase in range(3):
        bit = (code & (1 << (3 * direction + phase))) != 0
        up = [jnp.where(bit, mob_up[phase][s], mob_low[phase][s]) for s in range(3)]
        first = drop[0] if heads is None else drop[0] + trans * heads[phase]
        out.append(
            (
                up[0] * first,
                up[1] * first + up[0] * drop[1],
                up[2] * first + up[0] * drop[2],
            )
        )
    return out


def nine(p_ref, s_ref, ct_ref, at):
    return [
        p_ref[at, :], ct_ref[0, 0, at, :], ct_ref[1, 0, at, :],
        s_ref[0, at, :], ct_ref[0, 1, at, :], ct_ref[1, 1, at, :],
        s_ref[1, at, :], ct_ref[0, 2, at, :], ct_ref[1, 2, at, :],
    ]


def slot_kernel(p_ref, s_ref, ct_ref, sp_ref, st_ref, pc_ref, ps_ref, wi_ref, cnt_ref, pay_ref, slot_ref):
    at = pl.ds(0, CELL_ROWS)
    hi, lo = split(jnp.concatenate(nine(p_ref, s_ref, ct_ref, at), 0))
    raw = jnp.concatenate([hi, lo], 1)
    cell = pc_ref[...]
    lane = cell & (LANES - 1)
    row = cell >> 7
    lane_hot = one_hot(iota((LANES, SLOTS), 0) == lane)
    picked = jnp.dot(raw, jnp.concatenate([lane_hot, lane_hot], 0), preferred_element_type=F32)
    row_mask = iota((CELL_ROWS, SLOTS), 0) == row
    val = [
        jnp.sum(jnp.where(row_mask, picked[q * CELL_ROWS:(q + 1) * CELL_ROWS], 0.0), axis=0, keepdims=True)
        for q in range(9)
    ]
    owner = iota((TILES, SLOTS), 1) >> 4
    tile_hot = one_hot(iota((TILES, SLOTS), 0) == owner)
    counts = jnp.broadcast_to(cnt_ref[...].astype(F32).astype(BF16), (8, TILES))
    live = jnp.dot(counts, tile_hot, preferred_element_type=F32)[0:1]
    rank = (iota((1, SLOTS), 1) & (PEER - 1)).astype(F32)
    weight = jnp.where(rank < live, wi_ref[...], 0.0)
    press = val[0:3]
    mobility, _ = properties(press, val[3:6], val[6:9])
    wl = [[weight * mobility[a][s] for s in range(3)] for a in range(3)]
    total = [wl[0][s] + wl[1][s] + wl[2][s] for s in range(3)]
    carry = [
        total[0] * press[0],
        total[1] * press[0] + total[0] * press[1],
        total[2] * press[0] + total[0] * press[2],
    ]
    slot_ref[...] = jnp.concatenate(
        press + [wl[a][s] for s in range(3) for a in range(3)] + [jnp.zeros((4, SLOTS), F32)], 0
    )
    sent = jnp.concatenate(
        [ps_ref[...].astype(F32)] + carry + total + [jnp.zeros((1, SLOTS), F32)], 0
    )
    seg = [sp_ref[...], st_ref[0], st_ref[1]]
    for k in range(TILES):
        w = k // 8
        for s in range(3):
            pay_ref[k, s * 8:(s + 1) * 8, :] = seg[s]
        pay_ref[k, ROWS_A:ROWS_A + 8, :] = sent[:, w * LANES:(w + 1) * LANES]


def pack_kernel(p_ref, s_ref, ct_ref, t_ref, code_ref, well_ref, link_ref, xlo_ref, xhi_ref, ylo_ref, yhi_ref):
    first, last = pl.ds(0, NZ, stride=8), pl.ds(7, NZ, stride=8)
    for q, v in enumerate(nine(p_ref, s_ref, ct_ref, first)):
        xlo_ref[q * 8:(q + 1) * 8, :] = v
    for q, v in enumerate(nine(p_ref, s_ref, ct_ref, last)):
        xhi_ref[q * 8:(q + 1) * 8, :] = v
    well = well_ref[...].astype(F32)
    xlo_ref[72:80, :] = well
    xhi_ref[72:80, :] = t_ref[0, last, :]
    xhi_ref[80:88, :] = code_ref[last, :].astype(F32)
    xhi_ref[88:96, :] = well
    xhi_ref[96:104, :] = link_ref[...]
    lane = iota((8, LANES), 1)
    low = jnp.zeros((8, LANES), F32)
    high = jnp.zeros((8, LANES), F32)
    for z in range(NZ):
        at = pl.ds(z * 8, 8)
        for q, v in enumerate(nine(p_ref, s_ref, ct_ref, at)):
            c = q * 8 + z
            low = jnp.where(lane == c, roll(v, c, 1), low)
            high = jnp.where(lane == c, roll(v, c + 1, 1), high)
        high = jnp.where(lane == 72 + z, roll(t_ref[1, at, :], 73 + z, 1), high)
        high = jnp.where(lane == 80 + z, roll(code_ref[at, :].astype(F32), 81 + z, 1), high)
    ylo_ref[...] = low
    yhi_ref[...] = high


def stencil_kernel(p_ref, s_ref, ct_ref, om_ref, pv_ref, t_ref, code_ref, ylo_ref, yhi_ref,
                   exlo_ref, wxhi_ref, nylo_ref, syhi_ref, res_ref, prod_ref):
    top_x = lax.axis_index("xt") == TILES - 1
    top_y = lax.axis_index("yt") == lax.axis_size("yt") - 1
    lane = iota((8, LANES), 1)
    sub = iota((8, LANES), 0)

    half = lane < 64
    own_lo, own_hi, north, south = ylo_ref[...], yhi_ref[...], nylo_ref[...], syhi_ref[...]
    low = [jnp.where(half, roll(own_hi, -8 * q, 1), roll(south, 64 - 8 * q, 1)) for q in range(11)]
    up = [jnp.where(half, roll(north, -8 * q, 1), roll(own_lo, 64 - 8 * q, 1)) for q in range(9)]
    code_y = low[10].astype(jnp.int32)
    trans_y = jnp.where(jnp.logical_and(half, top_y), 0.0, low[9])
    rim = fluxes(
        properties(low[0:3], low[3:6], low[6:9])[0], properties(up[0:3], up[3:6], up[6:9])[0],
        low[0:3], up[0:3], trans_y, code_y, 1, None,
    )
    even = (lane & 1) == 0
    edge = jnp.logical_or(lane == 0, lane == LANES - 1)
    rim_even, rim_odd = [], []
    for a in range(3):
        moved = [roll(rim[a][s], 65, 1) for s in range(3)]
        rim_even.append([jnp.where(even, rim[a][s], -moved[s]) for s in range(3)])
        rim_odd.append([jnp.where(even, -moved[s], rim[a][s]) for s in range(3)])

    def put(s, a, at, value):
        if s == 0:
            res_ref[a, at, :] = value
        else:
            prod_ref[s - 1, a, at, :] = value

    def take(s, a, at):
        return res_ref[a, at, :] if s == 0 else prod_ref[s - 1, a, at, :]

    raw = nine(p_ref, s_ref, ct_ref, pl.ds(0, 8))
    mob, mass = properties(raw[0:3], raw[3:6], raw[6:9])
    press = raw[0:3]
    above = None
    for z in range(NZ):
        at = pl.ds(z * 8, 8)
        code = code_ref[at, :]
        volume = pv_ref[at, :]
        bal = [[volume * mass[a][s] for s in range(3)] for a in range(3)]
        for a in range(3):
            bal[a][0] = bal[a][0] - om_ref[a, at, :]
        for direction, axis, last in ((0, 0, sub == 7), (1, 1, lane == LANES - 1)):
            trans = jnp.where(last, 0.0, t_ref[direction, at, :])
            up_mob = [[roll(mob[a][s], -1, axis) for s in range(3)] for a in range(3)]
            up_press = [roll(press[s], -1, axis) for s in range(3)]
            flux = fluxes(mob, up_mob, press, up_press, trans, code, direction, None)
            for a in range(3):
                for s in range(3):
                    bal[a][s] = bal[a][s] + (flux[a][s] - roll(flux[a][s], 1, axis))
        rim_z = rim_even if z % 2 == 0 else rim_odd
        for a in range(3):
            for s in range(3):
                bal[a][s] = bal[a][s] + jnp.where(edge, roll(rim_z[a][s], LANES - 1 - z, 1), 0.0)
        if above is not None:
            for a in range(3):
                for s in range(3):
                    bal[a][s] = bal[a][s] - above[a][s]
        if z < NZ - 1:
            raw = nine(p_ref, s_ref, ct_ref, pl.ds(z * 8 + 8, 8))
            mob_next, mass = properties(raw[0:3], raw[3:6], raw[6:9])
            above = fluxes(mob, mob_next, press, raw[0:3], t_ref[2, at, :], code, 2, GRAVITY_HEAD)
            for a in range(3):
                for s in range(3):
                    bal[a][s] = bal[a][s] + above[a][s]
            mob, press = mob_next, raw[0:3]
        for a in range(3):
            for s in range(3):
                put(s, a, at, bal[a][s])

    first, last = pl.ds(0, NZ, stride=8), pl.ds(7, NZ, stride=8)

    def face(low, up, trans, code):
        return fluxes(
            properties(low[0:3], low[3:6], low[6:9])[0], properties(up[0:3], up[3:6], up[6:9])[0],
            low[0:3], up[0:3], trans, code, 0, None,
        )

    east = [exlo_ref[q * 8:(q + 1) * 8, :] for q in range(9)]
    flux = face(nine(p_ref, s_ref, ct_ref, last), east, jnp.where(top_x, 0.0, t_ref[0, last, :]), code_ref[last, :])
    for a in range(3):
        for s in range(3):
            put(s, a, last, take(s, a, last) + flux[a][s])
    west = [wxhi_ref[q * 8:(q + 1) * 8, :] for q in range(11)]
    flux = face(west[0:9], nine(p_ref, s_ref, ct_ref, first), west[9], west[10].astype(jnp.int32))
    for a in range(3):
        for s in range(3):
            put(s, a, first, take(s, a, first) - flux[a][s])


def join_kernel(got_ref, slot_ref, pc_ref, ps_ref, sp_ref, st_ref, well_ref, link_ref, heel_ref, exlo_ref, wxhi_ref,
                res_in, prod_in, res_ref, prod_ref, seg_ref):
    here = lax.axis_index("xt")
    lane = iota((8, LANES), 1)
    group = iota((1, LANES), 1) >> 4

    seg_number = ps_ref[...]
    seg_lane = seg_number & (LANES - 1)
    seg_row = seg_number >> 7
    rates = [[] for _ in range(9)]
    for w in range(4):
        cols = slice(w * LANES, (w + 1) * LANES)
        hot = one_hot(iota((LANES, LANES), 0) == seg_lane[:, cols])
        hi, lo = split(got_ref[w * 8:(w + 1) * 8, 0:ROWS_A, :].reshape(8 * ROWS_A, LANES))
        picked = jnp.dot(
            jnp.concatenate([hi, lo], 1), jnp.concatenate([hot, hot], 0), preferred_element_type=F32
        ).reshape(8, ROWS_A, LANES)
        mine = jnp.where(group == 0, picked[0], 0.0)
        for k in range(1, 8):
            mine = jnp.where(group == k, picked[k], mine)
        row_mask = iota((8, LANES), 0) == seg_row[:, cols]
        at_seg = [
            jnp.sum(jnp.where(row_mask, mine[s * 8:(s + 1) * 8], 0.0), axis=0, keepdims=True) for s in range(3)
        ]
        drop = [slot_ref[s:s + 1, cols] - at_seg[s] for s in range(3)]
        base = [slot_ref[3 + a:4 + a, cols] for a in range(3)]
        for a in range(3):
            rates[a].append(base[a] * drop[0])
            for s in (1, 2):
                r = 3 + s * 3 + a
                rates[s * 3 + a].append(slot_ref[r:r + 1, cols] * drop[0] + base[a] * drop[s])

    cell = pc_ref[...]
    lane_hot = one_hot(iota((LANES, SLOTS), 0) == (cell & (LANES - 1)))
    row_hot = one_hot(iota((CELL_ROWS, SLOTS), 0) == (cell >> 7))
    parts = [split(jnp.concatenate(r, 1)) for r in rates]
    left = jnp.concatenate(
        [jnp.concatenate([row_hot * hi, row_hot * lo], 1) for hi, lo in parts], 0
    )
    added = lax.dot_general(
        left, jnp.concatenate([lane_hot, lane_hot], 1), (((1,), (1,)), ((), ())), preferred_element_type=F32
    )
    for s in range(3):
        for a in range(3):
            n = s * 3 + a
            more = added[n * CELL_ROWS:(n + 1) * CELL_ROWS]
            if s == 0:
                res_ref[a] = res_in[a] + more
            else:
                prod_ref[s - 1, a] = prod_in[s - 1, a] + more

    turn = here & 7
    windows = []
    for w in range(4):
        acc = jnp.zeros((8, LANES), F32)
        for k in range(8):
            tile = got_ref[w * 8 + k, ROWS_A:ROWS_A + 8, :]
            shift = ((k - turn + 8) & 7) * PEER
            acc = jnp.where(group == k, pltpu.roll(tile, shift, 1), acc)
        windows.append(acc)
    told = jnp.concatenate(windows, 1)
    number = told[0:1].astype(jnp.int32)
    hot = one_hot(iota((LANES, SLOTS), 0) == (number & (LANES - 1)))
    row_mask = iota((8, SLOTS), 0) == (number >> 7)
    hi, lo = split(jnp.concatenate([jnp.where(row_mask, told[q:q + 1], 0.0) for q in range(1, 7)], 0))
    sums = lax.dot_general(
        jnp.concatenate([hi, lo], 1), jnp.concatenate([hot, hot], 1), (((1,), (1,)), ((), ())),
        preferred_element_type=F32,
    )
    c = [sums[s * 8:(s + 1) * 8] for s in range(3)]
    a = [sums[24 + s * 8:32 + s * 8] for s in range(3)]
    seg = [sp_ref[...], st_ref[0], st_ref[1]]
    inflow = [
        c[0] - seg[0] * a[0],
        c[1] - seg[0] * a[1] - seg[1] * a[0],
        c[2] - seg[0] * a[2] - seg[2] * a[0],
    ]

    after, before = (here + 1) % TILES, (here + TILES - 1) % TILES
    well = well_ref[...].astype(F32)
    link = link_ref[...]
    lane0 = lane == 0
    next_well = roll(jnp.where(lane0, exlo_ref[72:80, :], well), -1, 1)
    linked = jnp.logical_and(
        next_well == well, jnp.logical_not(jnp.logical_and(here == TILES - 1, lane == LANES - 1))
    )
    joined = jnp.logical_and(roll(wxhi_ref[88:96, :], 1, 1) == well, here > 0)
    link_west = roll(wxhi_ref[96:104, :], 1, 1)
    east = got_ref[after, 0:ROWS_A, :]
    west = got_ref[before, 0:ROWS_A, :]
    for s in range(3):
        part = slice(s * 8, (s + 1) * 8)
        next_press = roll(jnp.where(lane0, east[part], seg[s]), -1, 1)
        end = heel_ref[...] if s == 0 else jnp.zeros((8, LANES), F32)
        flow = link * (seg[s] - jnp.where(linked, next_press, end))
        carried = jnp.where(linked, flow, 0.0)
        entering = jnp.where(joined, link_west * (roll(west[part], 1, 1) - seg[s]), 0.0)
        seg_ref[s] = inflow[s] - flow + jnp.where(lane0, entering, roll(carried, 1, 1))


def call(kernel, out_shapes, *args, **kw):
    return pl.pallas_call(
        kernel,
        out_shape=[jax.ShapeDtypeStruct(s, F32) for s in out_shapes],
        in_specs=[VMEM] * len(args),
        out_specs=[VMEM] * len(out_shapes),
        compiler_params=pltpu.CompilerParams(vmem_limit_bytes=40 * 2**20),
        **kw,
    )(*args)


def shift(array, axis, by):
    length = lax.axis_size(axis)
    return lax.ppermute(array, axis, [(i, i + by) for i in range(length) if 0 <= i + by < length])


def body(
    pressure, saturation, old_mass, pore_volume, transmissibility, upwind_code, cell_tangent, segment_pressure,
    segment_tangent, segment_well, link_factor, heel_pressure, perforation_cell, perforation_segment, well_index,
    perforation_count,
):
    p = pressure.reshape(CELL_ROWS, LANES)
    sat = saturation.reshape(2, CELL_ROWS, LANES)
    om = old_mass.reshape(3, CELL_ROWS, LANES)
    pv = pore_volume.reshape(CELL_ROWS, LANES)
    tr = transmissibility.reshape(3, CELL_ROWS, LANES)
    code = upwind_code.reshape(CELL_ROWS, LANES)
    ct = cell_tangent.reshape(2, 3, CELL_ROWS, LANES)

    pay, slots = call(
        slot_kernel, [(TILES, 32, LANES), (16, SLOTS)],
        p, sat, ct, segment_pressure, segment_tangent, perforation_cell, perforation_segment, well_index,
        perforation_count,
    )
    got = lax.all_to_all(pay, "xt", 0, 0, tiled=True)
    xlo, xhi, ylo, yhi = call(
        pack_kernel, [(80, LANES), (104, LANES), (8, LANES), (8, LANES)],
        p, sat, ct, tr, code, segment_well, link_factor,
    )
    east_xlo = shift(xlo, "xt", -1)
    west_xhi = shift(xhi, "xt", 1)
    north_ylo = shift(ylo, "yt", -1)
    south_yhi = shift(yhi, "yt", 1)
    res, prod = call(
        stencil_kernel, [(3, CELL_ROWS, LANES), (2, 3, CELL_ROWS, LANES)],
        p, sat, ct, om, pv, tr, code, ylo, yhi, east_xlo, west_xhi, north_ylo, south_yhi,
    )
    res, prod, seg = call(
        join_kernel, [(3, CELL_ROWS, LANES), (2, 3, CELL_ROWS, LANES), (3, 8, LANES)],
        got, slots, perforation_cell, perforation_segment, segment_pressure, segment_tangent, segment_well,
        link_factor, heel_pressure, east_xlo, west_xhi, res, prod,
        input_output_aliases={11: 0, 12: 1},
    )
    return (res.reshape(old_mass.shape), prod.reshape(cell_tangent.shape), seg)


def solution(mesh):
    cell, seg = P(None, "xt", "yt"), P("yt", "xt")
    cell2, cell3, seg2 = P(None, None, "xt", "yt"), P(None, None, None, "xt", "yt"), P(None, "yt", "xt")
    in_specs = (
        cell, cell2, cell2, cell, cell2, cell, cell3, seg, seg2, seg, seg, seg, seg, seg, seg, seg,
    )
    return jax.shard_map(body, mesh=mesh, in_specs=in_specs, out_specs=(cell2, cell3, seg2), check_vma=False)
```

```python
import jax
import jax.numpy as jnp
from jax import lax
from jax.experimental import pallas as pl
from jax.experimental.pallas import tpu as pltpu
from jax.sharding import PartitionSpec as P

COMPRESS = (0.05, 0.1, 0.6)
INV_VISCOSITY = (2.0, 0.5, 5.0)
GRAVITY_HEAD = (0.3, 0.25, 0.05)

NZ = 8
LANES = 128
CELL_ROWS = 64
SLOTS = 512
TILES = 32
PEER = 16
ROWS_A = 24
BLOCK = ROWS_A + 1
F32 = jnp.float32
BF16 = jnp.bfloat16
VMEM = pl.BlockSpec(memory_space=pltpu.VMEM)


def roll(x, shift, axis):
    return pltpu.roll(x, shift % x.shape[axis], axis)


def iota(shape, dim):
    return lax.broadcasted_iota(jnp.int32, shape, dim)


def split(x):
    hi = x.astype(BF16)
    lo = (x - hi.astype(F32)).astype(BF16)
    return hi, lo


def one_hot(mask):
    return jnp.where(mask, 1.0, 0.0).astype(BF16)


def properties(press, water, gas):
    oil = (1.0 - water[0] - gas[0], -water[1] - gas[1], -water[2] - gas[2])
    mobility, mass = [], []
    for phase, sat in enumerate((water, oil, gas)):
        c = COMPRESS[phase]
        base = jnp.exp(c * press[0])
        cb = c * base
        m0 = base * sat[0]
        cs = cb * sat[0]
        m1 = cs * press[1] + base * sat[1]
        m2 = cs * press[2] + base * sat[2]
        v = INV_VISCOSITY[phase]
        vs = v * sat[0]
        vm = v * m0
        mobility.append((m0 * vs, m1 * vs + vm * sat[1], m2 * vs + vm * sat[2]))
        mass.append((m0, m1, m2))
    return mobility, mass


def fluxes(mob_low, mob_up, press_low, press_up, trans, code, direction, heads):
    drop = [trans * (press_low[s] - press_up[s]) for s in range(3)]
    out = []
    for phase in range(3):
        bit = (code & (1 << (3 * direction + phase))) != 0
        up = [jnp.where(bit, mob_up[phase][s], mob_low[phase][s]) for s in range(3)]
        first = drop[0] if heads is None else drop[0] + trans * heads[phase]
        out.append(
            (
                up[0] * first,
                up[1] * first + up[0] * drop[1],
                up[2] * first + up[0] * drop[2],
            )
        )
    return out


def nine(p_ref, s_ref, ct_ref, at):
    return [
        p_ref[at, :], ct_ref[0, 0, at, :], ct_ref[1, 0, at, :],
        s_ref[0, at, :], ct_ref[0, 1, at, :], ct_ref[1, 1, at, :],
        s_ref[1, at, :], ct_ref[0, 2, at, :], ct_ref[1, 2, at, :],
    ]


def exchange(x):
    sub, group = iota((8, LANES), 0), iota((8, LANES), 1) >> 4
    for b in (1, 2, 4):
        s, g = (sub & b) != 0, (group & b) != 0
        down = roll(roll(x, -b, 0), PEER * b, 1)
        up = roll(roll(x, b, 0), -PEER * b, 1)
        x = jnp.where(s == g, x, jnp.where(g, down, up))
    return x


def slot_kernel(p_hbm, s_hbm, ct_hbm, sp_hbm, st_hbm, pc_hbm, ps_hbm, wi_hbm, cnt_hbm, pay_ref, slot_ref,
                p_ref, s_ref, ct_ref, sp_ref, st_ref, pc_ref, ps_ref, wi_ref, cnt_ref, sems):
    pairs = [
        (p_hbm, p_ref), (s_hbm, s_ref), (ct_hbm, ct_ref), (pc_hbm, pc_ref), (sp_hbm, sp_ref), (st_hbm, st_ref),
        (ps_hbm, ps_ref), (wi_hbm, wi_ref), (cnt_hbm, cnt_ref),
    ]
    copies = [pltpu.make_async_copy(src, dst, sems.at[n]) for n, (src, dst) in enumerate(pairs)]
    for copy in copies:
        copy.start()
    for copy in copies:
        copy.wait()
    seg = [sp_ref[...], st_ref[0], st_ref[1]]
    for k in range(TILES):
        for s in range(3):
            pay_ref[pl.ds(k * BLOCK + s * 8, 8), :] = seg[s]
    at = pl.ds(0, CELL_ROWS)
    hi, lo = split(jnp.concatenate(nine(p_ref, s_ref, ct_ref, at), 0))
    raw = jnp.concatenate([hi, lo], 1)
    cell = pc_ref[...]
    lane = cell & (LANES - 1)
    row = cell >> 7
    lane_hot = one_hot(iota((LANES, SLOTS), 0) == lane)
    picked = jnp.dot(raw, jnp.concatenate([lane_hot, lane_hot], 0), preferred_element_type=F32)
    row_mask = iota((CELL_ROWS, SLOTS), 0) == row
    val = [
        jnp.sum(jnp.where(row_mask, picked[q * CELL_ROWS:(q + 1) * CELL_ROWS], 0.0), axis=0, keepdims=True)
        for q in range(9)
    ]
    owner = iota((TILES, SLOTS), 1) >> 4
    tile_hot = one_hot(iota((TILES, SLOTS), 0) == owner)
    counts = jnp.broadcast_to(cnt_ref[...].astype(F32).astype(BF16), (8, TILES))
    live = jnp.dot(counts, tile_hot, preferred_element_type=F32)[0:1]
    rank = (iota((1, SLOTS), 1) & (PEER - 1)).astype(F32)
    weight = jnp.where(rank < live, wi_ref[...], 0.0)
    press = val[0:3]
    mobility, _ = properties(press, val[3:6], val[6:9])
    wl = [[weight * mobility[a][s] for s in range(3)] for a in range(3)]
    total = [wl[0][s] + wl[1][s] + wl[2][s] for s in range(3)]
    carry = [
        total[0] * press[0],
        total[1] * press[0] + total[0] * press[1],
        total[2] * press[0] + total[0] * press[2],
    ]
    number = ps_ref[...].astype(F32)
    slot_ref[...] = jnp.concatenate(
        press + [wl[a][s] for s in range(3) for a in range(3)]
        + [cell.astype(F32), number, jnp.zeros((2, SLOTS), F32)], 0
    )
    sent = jnp.concatenate([number] + carry + total + [jnp.zeros((1, SLOTS), F32)], 0)
    for w in range(4):
        rows = exchange(sent[:, w * LANES:(w + 1) * LANES])
        for k in range(8):
            pay_ref[pl.ds((w * 8 + k) * BLOCK + ROWS_A, 1), :] = rows[k:k + 1]


def pack_kernel(p_ref, s_ref, ct_ref, t_ref, code_ref, sp_ref, st_ref, well_ref, link_ref, heel_ref,
                xlo_ref, xhi_ref, ylo_ref, yhi_ref, seg_ref):
    first, last = pl.ds(0, NZ, stride=8), pl.ds(7, NZ, stride=8)
    for q, v in enumerate(nine(p_ref, s_ref, ct_ref, first)):
        xlo_ref[q * 8:(q + 1) * 8, :] = v
    for q, v in enumerate(nine(p_ref, s_ref, ct_ref, last)):
        xhi_ref[q * 8:(q + 1) * 8, :] = v
    xhi_ref[72:80, :] = t_ref[0, last, :]
    xhi_ref[80:88, :] = code_ref[last, :].astype(F32)
    lane = iota((8, LANES), 1)
    seg = [well_ref[...].astype(F32), link_ref[...], sp_ref[...], st_ref[0], st_ref[1], heel_ref[...]]
    for n, v in enumerate(seg):
        seg_ref[n * 8:(n + 1) * 8, :] = v
    left, right = seg[0], seg[0]
    for n in range(1, 5):
        left = jnp.where(lane == n, roll(seg[n], n, 1), left)
        right = jnp.where(lane == LANES - 1 - n, roll(seg[n], -n, 1), right)
    xlo_ref[72:80, :] = left
    xhi_ref[88:96, :] = right
    low = jnp.zeros((8, LANES), F32)
    high = jnp.zeros((8, LANES), F32)
    for z in range(NZ):
        at = pl.ds(z * 8, 8)
        for q, v in enumerate(nine(p_ref, s_ref, ct_ref, at)):
            c = q * 8 + z
            low = jnp.where(lane == c, roll(v, c, 1), low)
            high = jnp.where(lane == c, roll(v, c + 1, 1), high)
        high = jnp.where(lane == 72 + z, roll(t_ref[1, at, :], 73 + z, 1), high)
        high = jnp.where(lane == 80 + z, roll(code_ref[at, :].astype(F32), 81 + z, 1), high)
    ylo_ref[...] = low
    yhi_ref[...] = high


def stencil_kernel(p_ref, s_ref, ct_ref, om_ref, pv_ref, t_ref, code_ref, bal_ref):
    lane = iota((8, LANES), 1)
    sub = iota((8, LANES), 0)
    raw = nine(p_ref, s_ref, ct_ref, pl.ds(0, 8))
    mob, mass = properties(raw[0:3], raw[3:6], raw[6:9])
    press = raw[0:3]
    above = None
    for z in range(NZ):
        at = pl.ds(z * 8, 8)
        code = code_ref[at, :]
        volume = pv_ref[at, :]
        bal = [[volume * mass[a][s] for s in range(3)] for a in range(3)]
        for a in range(3):
            bal[a][0] = bal[a][0] - om_ref[a, at, :]
        for direction, axis, last in ((0, 0, sub == 7), (1, 1, lane == LANES - 1)):
            trans = jnp.where(last, 0.0, t_ref[direction, at, :])
            up_mob = [[roll(mob[a][s], -1, axis) for s in range(3)] for a in range(3)]
            up_press = [roll(press[s], -1, axis) for s in range(3)]
            flux = fluxes(mob, up_mob, press, up_press, trans, code, direction, None)
            for a in range(3):
                for s in range(3):
                    bal[a][s] = bal[a][s] + (flux[a][s] - roll(flux[a][s], 1, axis))
        if above is not None:
            for a in range(3):
                for s in range(3):
                    bal[a][s] = bal[a][s] - above[a][s]
        if z < NZ - 1:
            raw = nine(p_ref, s_ref, ct_ref, pl.ds(z * 8 + 8, 8))
            mob_next, mass = properties(raw[0:3], raw[3:6], raw[6:9])
            above = fluxes(mob, mob_next, press, raw[0:3], t_ref[2, at, :], code, 2, GRAVITY_HEAD)
            for a in range(3):
                for s in range(3):
                    bal[a][s] = bal[a][s] + above[a][s]
            mob, press = mob_next, raw[0:3]
        for a in range(3):
            for s in range(3):
                bal_ref[s * 3 + a, at, :] = bal[a][s]


def face(low, up, trans, code, direction):
    return fluxes(
        properties(low[0:3], low[3:6], low[6:9])[0], properties(up[0:3], up[3:6], up[6:9])[0],
        low[0:3], up[0:3], trans, code, direction, None,
    )


def join_kernel(got_ref, slot_ref, bal_ref, seg_ref, xlo_ref, xhi_ref, ylo_ref, yhi_ref,
                exlo_ref, wxhi_ref, nylo_ref, syhi_ref, res_ref, prod_ref, segout_ref):
    top_x = lax.axis_index("xt") == TILES - 1
    top_y = lax.axis_index("yt") == lax.axis_size("yt") - 1
    lane = iota((8, LANES), 1)
    group = iota((1, LANES), 1) >> 4

    seg_number = slot_ref[13:14, :].astype(jnp.int32)
    seg_lane = seg_number & (LANES - 1)
    seg_row = seg_number >> 7
    rates = [[] for _ in range(9)]
    for w in range(4):
        cols = slice(w * LANES, (w + 1) * LANES)
        hot = one_hot(iota((LANES, LANES), 0) == seg_lane[:, cols])
        blocks = [got_ref[pl.ds((w * 8 + k) * BLOCK, ROWS_A), :] for k in range(8)]
        hi, lo = split(jnp.concatenate(blocks, 0))
        picked = jnp.dot(
            jnp.concatenate([hi, lo], 1), jnp.concatenate([hot, hot], 0), preferred_element_type=F32
        )
        mine = picked[0:ROWS_A]
        for k in range(1, 8):
            mine = jnp.where(group == k, picked[k * ROWS_A:(k + 1) * ROWS_A], mine)
        row_mask = iota((8, LANES), 0) == seg_row[:, cols]
        at_seg = [
            jnp.sum(jnp.where(row_mask, mine[s * 8:(s + 1) * 8], 0.0), axis=0, keepdims=True) for s in range(3)
        ]
        drop = [slot_ref[s:s + 1, cols] - at_seg[s] for s in range(3)]
        base = [slot_ref[3 + a:4 + a, cols] for a in range(3)]
        for a in range(3):
            rates[a].append(base[a] * drop[0])
            for s in (1, 2):
                r = 3 + s * 3 + a
                rates[s * 3 + a].append(slot_ref[r:r + 1, cols] * drop[0] + base[a] * drop[s])

    cell = slot_ref[12:13, :].astype(jnp.int32)
    lane_hot = one_hot(iota((LANES, SLOTS), 0) == (cell & (LANES - 1)))
    row_hot = one_hot(iota((CELL_ROWS, SLOTS), 0) == (cell >> 7))
    parts = [split(jnp.concatenate(r, 1)) for r in rates]
    left = jnp.concatenate(
        [jnp.concatenate([row_hot * hi, row_hot * lo], 1) for hi, lo in parts], 0
    )
    added = lax.dot_general(
        left, jnp.concatenate([lane_hot, lane_hot], 1), (((1,), (1,)), ((), ())), preferred_element_type=F32
    )

    half = lane < 64
    own_lo, own_hi, north, south = ylo_ref[...], yhi_ref[...], nylo_ref[...], syhi_ref[...]
    low = [jnp.where(half, roll(own_hi, -8 * q, 1), roll(south, 64 - 8 * q, 1)) for q in range(11)]
    up = [jnp.where(half, roll(north, -8 * q, 1), roll(own_lo, 64 - 8 * q, 1)) for q in range(9)]
    trans = jnp.where(jnp.logical_and(half, top_y), 0.0, low[9])
    rim = face(low[0:9], up, trans, low[10].astype(jnp.int32), 1)
    even = (lane & 1) == 0
    edge = jnp.logical_or(lane == 0, lane == LANES - 1)

    def planes(ref, count):
        return [ref[q * 8:(q + 1) * 8, :] for q in range(count)]

    own, near = planes(xhi_ref, 11), planes(wxhi_ref, 11)
    east = face(own[0:9], planes(exlo_ref, 9), jnp.where(top_x, 0.0, own[9]), own[10].astype(jnp.int32), 0)
    west = face(near[0:9], planes(xlo_ref, 9), near[9], near[10].astype(jnp.int32), 0)
    first, last = pl.ds(0, NZ, stride=8), pl.ds(7, NZ, stride=8)

    for s in range(3):
        for a in range(3):
            n = s * 3 + a
            flux = rim[a][s]
            moved = roll(flux, 65, 1)
            by_parity = (jnp.where(even, flux, -moved), jnp.where(even, -moved, flux))
            out = res_ref.at[a] if s == 0 else prod_ref.at[s - 1, a]
            for z in range(NZ):
                at = pl.ds(z * 8, 8)
                rim_z = jnp.where(edge, roll(by_parity[z % 2], LANES - 1 - z, 1), 0.0)
                out[at, :] = bal_ref[n, at, :] + added[n * CELL_ROWS + z * 8:n * CELL_ROWS + z * 8 + 8] + rim_z
            out[last, :] = out[last, :] + east[a][s]
            out[first, :] = out[first, :] - west[a][s]

    told = jnp.concatenate(
        [exchange(got_ref[pl.ds(w * 8 * BLOCK + ROWS_A, 8, stride=BLOCK), :]) for w in range(4)], 1
    )
    number = told[0:1].astype(jnp.int32)
    hot = one_hot(iota((LANES, SLOTS), 0) == (number & (LANES - 1)))
    row_mask = iota((8, SLOTS), 0) == (number >> 7)
    hi, lo = split(jnp.concatenate([jnp.where(row_mask, told[q:q + 1], 0.0) for q in range(1, 7)], 0))
    sums = lax.dot_general(
        jnp.concatenate([hi, lo], 1), jnp.concatenate([hot, hot], 1), (((1,), (1,)), ((), ())),
        preferred_element_type=F32,
    )
    c = [sums[s * 8:(s + 1) * 8] for s in range(3)]
    a = [sums[24 + s * 8:32 + s * 8] for s in range(3)]
    well, link, *seg = planes(seg_ref, 5)
    heel = seg_ref[40:48, :]
    inflow = [
        c[0] - seg[0] * a[0],
        c[1] - seg[0] * a[1] - seg[1] * a[0],
        c[2] - seg[0] * a[2] - seg[2] * a[0],
    ]

    after, before = exlo_ref[72:80, :], wxhi_ref[88:96, :]
    lane0 = lane == 0
    next_well = roll(jnp.where(lane0, after, well), -1, 1)
    linked = jnp.logical_and(next_well == well, jnp.logical_not(jnp.logical_and(top_x, lane == LANES - 1)))
    joined = roll(before, 1, 1) == well
    link_west = roll(before, 2, 1)
    for s in range(3):
        next_press = roll(jnp.where(lane0, roll(after, -2 - s, 1), seg[s]), -1, 1)
        end = heel if s == 0 else jnp.zeros((8, LANES), F32)
        flow = link * (seg[s] - jnp.where(linked, next_press, end))
        carried = jnp.where(linked, flow, 0.0)
        entering = jnp.where(joined, link_west * (roll(before, 3 + s, 1) - seg[s]), 0.0)
        segout_ref[s] = inflow[s] - flow + jnp.where(lane0, entering, roll(carried, 1, 1))


def call(kernel, out_shapes, *args, in_spec=VMEM, scratch=()):
    return pl.pallas_call(
        kernel,
        out_shape=[jax.ShapeDtypeStruct(s, F32) for s in out_shapes],
        in_specs=[in_spec] * len(args),
        out_specs=[VMEM] * len(out_shapes),
        scratch_shapes=scratch,
        compiler_params=pltpu.CompilerParams(vmem_limit_bytes=16 * 2**20),
    )(*args)


def call_loading(kernel, out_shapes, *args):
    scratch = [pltpu.VMEM(a.shape, a.dtype) for a in args] + [pltpu.SemaphoreType.DMA((len(args),))]
    args = [pltpu.with_memory_space_constraint(a, pltpu.HBM) for a in args]
    return call(kernel, out_shapes, *args, in_spec=pl.BlockSpec(memory_space=pltpu.HBM), scratch=scratch)


def shift(array, axis, by):
    length = lax.axis_size(axis)
    return lax.ppermute(array, axis, [(i, i + by) for i in range(length) if 0 <= i + by < length])


def body(
    pressure, saturation, old_mass, pore_volume, transmissibility, upwind_code, cell_tangent, segment_pressure,
    segment_tangent, segment_well, link_factor, heel_pressure, perforation_cell, perforation_segment, well_index,
    perforation_count,
):
    p = pressure.reshape(CELL_ROWS, LANES)
    sat = saturation.reshape(2, CELL_ROWS, LANES)
    om = old_mass.reshape(3, CELL_ROWS, LANES)
    pv = pore_volume.reshape(CELL_ROWS, LANES)
    tr = transmissibility.reshape(3, CELL_ROWS, LANES)
    code = upwind_code.reshape(CELL_ROWS, LANES)
    ct = cell_tangent.reshape(2, 3, CELL_ROWS, LANES)

    pay, slots = call_loading(
        slot_kernel, [(TILES * BLOCK, LANES), (16, SLOTS)],
        p, sat, ct, segment_pressure, segment_tangent, perforation_cell, perforation_segment, well_index,
        perforation_count,
    )
    got = lax.all_to_all(pay.reshape(TILES, 1, BLOCK * LANES), "xt", 0, 0, tiled=True)
    got = got.reshape(TILES * BLOCK, LANES)
    xlo, xhi, ylo, yhi, seg = call(
        pack_kernel, [(80, LANES), (96, LANES), (8, LANES), (8, LANES), (48, LANES)],
        p, sat, ct, tr, code, segment_pressure, segment_tangent, segment_well, link_factor, heel_pressure,
    )
    west_xhi = shift(xhi, "xt", 1)
    east_xlo = shift(xlo, "xt", -1)
    north_ylo = shift(ylo, "yt", -1)
    south_yhi = shift(yhi, "yt", 1)
    (bal,) = call(stencil_kernel, [(9, CELL_ROWS, LANES)], p, sat, ct, om, pv, tr, code)
    res, prod, seg = call(
        join_kernel, [(3, CELL_ROWS, LANES), (2, 3, CELL_ROWS, LANES), (3, 8, LANES)],
        got, slots, bal, seg, xlo, xhi, ylo, yhi, east_xlo, west_xhi, north_ylo, south_yhi,
    )
    return (res.reshape(old_mass.shape), prod.reshape(cell_tangent.shape), seg)


def solution(mesh):
    cell, seg = P(None, "xt", "yt"), P("yt", "xt")
    cell2, cell3, seg2 = P(None, None, "xt", "yt"), P(None, None, None, "xt", "yt"), P(None, "yt", "xt")
    in_specs = (
        cell, cell2, cell2, cell, cell2, cell, cell3, seg, seg2, seg, seg, seg, seg, seg, seg, seg,
    )
    return jax.shard_map(body, mesh=mesh, in_specs=in_specs, out_specs=(cell2, cell3, seg2), check_vma=False)
```

```python
import jax
import jax.numpy as jnp
from jax import lax
from jax.experimental import pallas as pl
from jax.experimental.pallas import tpu as pltpu
from jax.sharding import PartitionSpec as P

COMPRESS = (0.05, 0.1, 0.6)
INV_VISCOSITY = (2.0, 0.5, 5.0)
GRAVITY_HEAD = (0.3, 0.25, 0.05)

NZ = 8
LANES = 128
CELL_ROWS = 64
SLOTS = 512
TILES = 32
PEER = 16
ROWS_A = 24
BLOCK = ROWS_A + 1
WIDE = 256
WIDE_ROWS = 32
F32 = jnp.float32
BF16 = jnp.bfloat16
VMEM = pl.BlockSpec(memory_space=pltpu.VMEM)


def roll(x, shift, axis):
    return pltpu.roll(x, shift % x.shape[axis], axis)


def iota(shape, dim):
    return lax.broadcasted_iota(jnp.int32, shape, dim)


def split(x):
    hi = x.astype(BF16)
    lo = (x - hi.astype(F32)).astype(BF16)
    return hi, lo


def one_hot(mask):
    return jnp.where(mask, 1.0, 0.0).astype(BF16)


def properties(press, water, gas):
    oil = (1.0 - water[0] - gas[0], -water[1] - gas[1], -water[2] - gas[2])
    mobility, mass = [], []
    for phase, sat in enumerate((water, oil, gas)):
        c = COMPRESS[phase]
        base = jnp.exp(c * press[0])
        cb = c * base
        m0 = base * sat[0]
        cs = cb * sat[0]
        m1 = cs * press[1] + base * sat[1]
        m2 = cs * press[2] + base * sat[2]
        v = INV_VISCOSITY[phase]
        vs = v * sat[0]
        vm = v * m0
        mobility.append((m0 * vs, m1 * vs + vm * sat[1], m2 * vs + vm * sat[2]))
        mass.append((m0, m1, m2))
    return mobility, mass


def fluxes(mob_low, mob_up, press_low, press_up, trans, code, direction, heads):
    drop = [trans * (press_low[s] - press_up[s]) for s in range(3)]
    out = []
    for phase in range(3):
        bit = (code & (1 << (3 * direction + phase))) != 0
        up = [jnp.where(bit, mob_up[phase][s], mob_low[phase][s]) for s in range(3)]
        first = drop[0] if heads is None else drop[0] + trans * heads[phase]
        out.append(
            (
                up[0] * first,
                up[1] * first + up[0] * drop[1],
                up[2] * first + up[0] * drop[2],
            )
        )
    return out


def nine(p_ref, s_ref, ct_ref, at):
    return [
        p_ref[at, :], ct_ref[0, 0, at, :], ct_ref[1, 0, at, :],
        s_ref[0, at, :], ct_ref[0, 1, at, :], ct_ref[1, 1, at, :],
        s_ref[1, at, :], ct_ref[0, 2, at, :], ct_ref[1, 2, at, :],
    ]


def exchange(x):
    sub, group = iota((8, LANES), 0), iota((8, LANES), 1) >> 4
    for b in (1, 2, 4):
        s, g = (sub & b) != 0, (group & b) != 0
        down = roll(roll(x, -b, 0), PEER * b, 1)
        up = roll(roll(x, b, 0), -PEER * b, 1)
        x = jnp.where(s == g, x, jnp.where(g, down, up))
    return x


def planes(ref, count):
    return [ref[q * 8:(q + 1) * 8, :] for q in range(count)]


def slot_kernel(p_hbm, s_hbm, ct_hbm, sp_hbm, st_hbm, pc_hbm, ps_hbm, wi_hbm, cnt_hbm, pay_ref, slot_ref,
                p_ref, s_ref, ct_ref, sp_ref, st_ref, pc_ref, ps_ref, wi_ref, cnt_ref, sems):
    pairs = [
        (pc_hbm, pc_ref), (sp_hbm, sp_ref), (st_hbm, st_ref), (cnt_hbm, cnt_ref), (wi_hbm, wi_ref), (ps_hbm, ps_ref),
        (p_hbm, p_ref), (s_hbm, s_ref), (ct_hbm, ct_ref),
    ]
    copies = [pltpu.make_async_copy(src, dst, sems.at[n]) for n, (src, dst) in enumerate(pairs)]
    for copy in copies:
        copy.start()
    owner = iota((TILES, SLOTS), 1) >> 4
    tile_hot = one_hot(iota((TILES, SLOTS), 0) == owner)
    copies[0].wait()
    cell = pc_ref[...]
    lane_hot = one_hot(iota((LANES, SLOTS), 0) == (cell & (LANES - 1)))
    lane_hot = jnp.concatenate([lane_hot, lane_hot], 0)
    row_mask = iota((CELL_ROWS, SLOTS), 0) == (cell >> 7)
    for copy in copies[1:6]:
        copy.wait()
    seg = [sp_ref[...], st_ref[0], st_ref[1]]
    for k in range(TILES):
        for s in range(3):
            pay_ref[pl.ds(k * BLOCK + s * 8, 8), :] = seg[s]
    counts = jnp.broadcast_to(cnt_ref[...].astype(F32).astype(BF16), (8, TILES))
    live = jnp.dot(counts, tile_hot, preferred_element_type=F32)[0:1]
    rank = (iota((1, SLOTS), 1) & (PEER - 1)).astype(F32)
    weight = jnp.where(rank < live, wi_ref[...], 0.0)
    number = ps_ref[...].astype(F32)
    for copy in copies[6:]:
        copy.wait()
    at = pl.ds(0, CELL_ROWS)
    hi, lo = split(jnp.concatenate(nine(p_ref, s_ref, ct_ref, at), 0))
    picked = jnp.dot(jnp.concatenate([hi, lo], 1), lane_hot, preferred_element_type=F32)
    val = [
        jnp.sum(jnp.where(row_mask, picked[q * CELL_ROWS:(q + 1) * CELL_ROWS], 0.0), axis=0, keepdims=True)
        for q in range(9)
    ]
    press = val[0:3]
    mobility, _ = properties(press, val[3:6], val[6:9])
    wl = [[weight * mobility[a][s] for s in range(3)] for a in range(3)]
    total = [wl[0][s] + wl[1][s] + wl[2][s] for s in range(3)]
    carry = [
        total[0] * press[0],
        total[1] * press[0] + total[0] * press[1],
        total[2] * press[0] + total[0] * press[2],
    ]
    sent = jnp.concatenate([number] + carry + total + [jnp.zeros((1, SLOTS), F32)], 0)
    for w in range(4):
        rows = exchange(sent[:, w * LANES:(w + 1) * LANES])
        for k in range(8):
            pay_ref[pl.ds((w * 8 + k) * BLOCK + ROWS_A, 1), :] = rows[k:k + 1]
    slot_ref[...] = jnp.concatenate(
        press + [wl[a][s] for s in range(3) for a in range(3)]
        + [cell.astype(F32), number, jnp.zeros((2, SLOTS), F32)], 0
    )


def pack_kernel(p_ref, s_ref, ct_ref, t_ref, code_ref, sp_ref, st_ref, well_ref, link_ref, heel_ref,
                xlo_ref, xhi_ref, ylo_ref, yhi_ref, seg_ref):
    first, last = pl.ds(0, NZ, stride=8), pl.ds(7, NZ, stride=8)
    for q, v in enumerate(nine(p_ref, s_ref, ct_ref, first)):
        xlo_ref[q * 8:(q + 1) * 8, :] = v
    for q, v in enumerate(nine(p_ref, s_ref, ct_ref, last)):
        xhi_ref[q * 8:(q + 1) * 8, :] = v
    xhi_ref[72:80, :] = t_ref[0, last, :]
    xhi_ref[80:88, :] = code_ref[last, :].astype(F32)
    lane = iota((8, LANES), 1)
    seg = [well_ref[...].astype(F32), link_ref[...], sp_ref[...], st_ref[0], st_ref[1], heel_ref[...]]
    for n, v in enumerate(seg):
        seg_ref[n * 8:(n + 1) * 8, :] = v
    left, right = seg[0], seg[0]
    for n in range(1, 5):
        left = jnp.where(lane == n, roll(seg[n], n, 1), left)
        right = jnp.where(lane == LANES - 1 - n, roll(seg[n], -n, 1), right)
    xlo_ref[72:80, :] = left
    xhi_ref[88:96, :] = right
    low = jnp.zeros((8, LANES), F32)
    high = jnp.zeros((8, LANES), F32)
    for z in range(NZ):
        at = pl.ds(z * 8, 8)
        for q, v in enumerate(nine(p_ref, s_ref, ct_ref, at)):
            c = q * 8 + z
            low = jnp.where(lane == c, roll(v, c, 1), low)
            high = jnp.where(lane == c, roll(v, c + 1, 1), high)
        high = jnp.where(lane == 72 + z, roll(t_ref[1, at, :], 73 + z, 1), high)
        high = jnp.where(lane == 80 + z, roll(code_ref[at, :].astype(F32), 81 + z, 1), high)
    ylo_ref[...] = low
    yhi_ref[...] = high


def face(low, up, trans, code, direction):
    return fluxes(
        properties(low[0:3], low[3:6], low[6:9])[0], properties(up[0:3], up[3:6], up[6:9])[0],
        low[0:3], up[0:3], trans, code, direction, None,
    )


def stencil_kernel(p_ref, s_ref, ct_ref, om_ref, pv_ref, t_ref, code_ref, slot_ref, xlo_ref, xhi_ref, exlo_ref, wxhi_ref,
                   bal_ref, lane_hot_ref, row_hot_ref, seg_hot_ref):
    cell = slot_ref[12:13, :].astype(jnp.int32)
    lane_hot = jnp.where(iota((WIDE, SLOTS), 0) == (cell & (WIDE - 1)), 1.0, 0.0).T.astype(BF16)
    lane_hot_ref[0:SLOTS, :] = lane_hot
    lane_hot_ref[SLOTS:2 * SLOTS, :] = lane_hot
    row_hot_ref[...] = one_hot(iota((WIDE_ROWS, SLOTS), 0) == (cell >> 8))
    seg_lane = slot_ref[13:14, :].astype(jnp.int32) & (LANES - 1)
    for w in range(4):
        hot = one_hot(iota((LANES, LANES), 0) == seg_lane[:, w * LANES:(w + 1) * LANES])
        seg_hot_ref[w, 0:LANES, :] = hot
        seg_hot_ref[w, LANES:2 * LANES, :] = hot
    lane = iota((8, LANES), 1)
    sub = iota((8, LANES), 0)
    raw = nine(p_ref, s_ref, ct_ref, pl.ds(0, 8))
    mob, mass = properties(raw[0:3], raw[3:6], raw[6:9])
    press = raw[0:3]
    above = None
    for z in range(NZ):
        at = pl.ds(z * 8, 8)
        code = code_ref[at, :]
        volume = pv_ref[at, :]
        bal = [[volume * mass[a][s] for s in range(3)] for a in range(3)]
        for a in range(3):
            bal[a][0] = bal[a][0] - om_ref[a, at, :]
        for direction, axis, last in ((0, 0, sub == 7), (1, 1, lane == LANES - 1)):
            trans = jnp.where(last, 0.0, t_ref[direction, at, :])
            up_mob = [[roll(mob[a][s], -1, axis) for s in range(3)] for a in range(3)]
            up_press = [roll(press[s], -1, axis) for s in range(3)]
            flux = fluxes(mob, up_mob, press, up_press, trans, code, direction, None)
            for a in range(3):
                for s in range(3):
                    bal[a][s] = bal[a][s] + (flux[a][s] - roll(flux[a][s], 1, axis))
        if above is not None:
            for a in range(3):
                for s in range(3):
                    bal[a][s] = bal[a][s] - above[a][s]
        if z < NZ - 1:
            raw = nine(p_ref, s_ref, ct_ref, pl.ds(z * 8 + 8, 8))
            mob_next, mass = properties(raw[0:3], raw[3:6], raw[6:9])
            above = fluxes(mob, mob_next, press, raw[0:3], t_ref[2, at, :], code, 2, GRAVITY_HEAD)
            for a in range(3):
                for s in range(3):
                    bal[a][s] = bal[a][s] + above[a][s]
            mob, press = mob_next, raw[0:3]
        for a in range(3):
            for s in range(3):
                bal_ref[s * 3 + a, at, :] = bal[a][s]

    top_x = lax.axis_index("xt") == TILES - 1
    own, near = planes(xhi_ref, 11), planes(wxhi_ref, 11)
    east = face(own[0:9], planes(exlo_ref, 9), jnp.where(top_x, 0.0, own[9]), own[10].astype(jnp.int32), 0)
    west = face(near[0:9], planes(xlo_ref, 9), near[9], near[10].astype(jnp.int32), 0)
    first, last = pl.ds(0, NZ, stride=8), pl.ds(7, NZ, stride=8)
    for s in range(3):
        for a in range(3):
            n = s * 3 + a
            bal_ref[n, last, :] = bal_ref[n, last, :] + east[a][s]
            bal_ref[n, first, :] = bal_ref[n, first, :] - west[a][s]


def join_kernel(got_ref, slot_ref, bal_ref, seg_ref, lane_hot_ref, row_hot_ref, seg_hot_ref, ylo_ref, yhi_ref,
                nylo_ref, syhi_ref, exlo_ref, wxhi_ref, res_hbm, prod_hbm, segout_hbm, out_ref, segout_ref, sems):
    top_x = lax.axis_index("xt") == TILES - 1
    top_y = lax.axis_index("yt") == lax.axis_size("yt") - 1
    lane = iota((8, LANES), 1)
    group = iota((1, LANES), 1) >> 4

    half = lane < 64
    own_lo, own_hi, north, south = ylo_ref[...], yhi_ref[...], nylo_ref[...], syhi_ref[...]
    low = [jnp.where(half, roll(own_hi, -8 * q, 1), roll(south, 64 - 8 * q, 1)) for q in range(11)]
    up = [jnp.where(half, roll(north, -8 * q, 1), roll(own_lo, 64 - 8 * q, 1)) for q in range(9)]
    trans = jnp.where(jnp.logical_and(half, top_y), 0.0, low[9])
    rim = face(low[0:9], up, trans, low[10].astype(jnp.int32), 1)
    even = (lane & 1) == 0
    edge = jnp.logical_or(lane == 0, lane == LANES - 1)

    seg_row = slot_ref[13:14, :].astype(jnp.int32) >> 7
    rates = [[] for _ in range(9)]
    for w in range(4):
        cols = slice(w * LANES, (w + 1) * LANES)
        blocks = [got_ref[pl.ds((w * 8 + k) * BLOCK, ROWS_A), :] for k in range(8)]
        hi, lo = split(jnp.concatenate(blocks, 0))
        picked = jnp.dot(jnp.concatenate([hi, lo], 1), seg_hot_ref[w], preferred_element_type=F32)
        mine = picked[0:ROWS_A]
        for k in range(1, 8):
            mine = jnp.where(group == k, picked[k * ROWS_A:(k + 1) * ROWS_A], mine)
        row_mask = iota((8, LANES), 0) == seg_row[:, cols]
        at_seg = [
            jnp.sum(jnp.where(row_mask, mine[s * 8:(s + 1) * 8], 0.0), axis=0, keepdims=True) for s in range(3)
        ]
        drop = [slot_ref[s:s + 1, cols] - at_seg[s] for s in range(3)]
        base = [slot_ref[3 + a:4 + a, cols] for a in range(3)]
        for a in range(3):
            rates[a].append(base[a] * drop[0])
            for s in (1, 2):
                r = 3 + s * 3 + a
                rates[s * 3 + a].append(slot_ref[r:r + 1, cols] * drop[0] + base[a] * drop[s])

    row_hot = row_hot_ref[...]
    parts = [split(jnp.concatenate(r, 1)) for r in rates]
    left = jnp.concatenate([jnp.concatenate([row_hot * hi, row_hot * lo], 1) for hi, lo in parts], 0)
    added = jnp.dot(left, lane_hot_ref[...], preferred_element_type=F32)
    copies = []
    for s in range(3):
        for a in range(3):
            n = s * 3 + a
            flux = rim[a][s]
            moved = roll(flux, 65, 1)
            by_parity = (jnp.where(even, flux, -moved), jnp.where(even, -moved, flux))
            for z in range(NZ):
                at = pl.ds(z * 8, 8)
                out_ref[n, at, :] = bal_ref[n, at, :] + jnp.where(
                    edge, roll(by_parity[z % 2], LANES - 1 - z, 1), 0.0
                )
            for h in range(2):
                at = pl.ds(h, WIDE_ROWS, stride=2)
                more = added[n * WIDE_ROWS:(n + 1) * WIDE_ROWS, h * LANES:(h + 1) * LANES]
                out_ref[n, at, :] = out_ref[n, at, :] + more
        copies.append(pltpu.make_async_copy(
            out_ref.at[pl.ds(s * 3, 3)], res_hbm if s == 0 else prod_hbm.at[s - 1], sems.at[s]
        ))
        copies[-1].start()

    told = jnp.concatenate(
        [exchange(got_ref[pl.ds(w * 8 * BLOCK + ROWS_A, 8, stride=BLOCK), :]) for w in range(4)], 1
    )
    number = told[0:1].astype(jnp.int32)
    hot = one_hot(iota((LANES, SLOTS), 0) == (number & (LANES - 1)))
    row_mask = iota((8, SLOTS), 0) == (number >> 7)
    hi, lo = split(jnp.concatenate([jnp.where(row_mask, told[q:q + 1], 0.0) for q in range(1, 7)], 0))
    sums = lax.dot_general(
        jnp.concatenate([hi, lo], 1), jnp.concatenate([hot, hot], 1), (((1,), (1,)), ((), ())),
        preferred_element_type=F32,
    )
    c = [sums[s * 8:(s + 1) * 8] for s in range(3)]
    a = [sums[24 + s * 8:32 + s * 8] for s in range(3)]
    well, link, *seg = planes(seg_ref, 5)
    heel = seg_ref[40:48, :]
    inflow = [
        c[0] - seg[0] * a[0],
        c[1] - seg[0] * a[1] - seg[1] * a[0],
        c[2] - seg[0] * a[2] - seg[2] * a[0],
    ]

    after, before = exlo_ref[72:80, :], wxhi_ref[88:96, :]
    lane0 = lane == 0
    next_well = roll(jnp.where(lane0, after, well), -1, 1)
    linked = jnp.logical_and(next_well == well, jnp.logical_not(jnp.logical_and(top_x, lane == LANES - 1)))
    joined = roll(before, 1, 1) == well
    link_west = roll(before, 2, 1)
    for s in range(3):
        next_press = roll(jnp.where(lane0, roll(after, -2 - s, 1), seg[s]), -1, 1)
        end = heel if s == 0 else jnp.zeros((8, LANES), F32)
        flow = link * (seg[s] - jnp.where(linked, next_press, end))
        carried = jnp.where(linked, flow, 0.0)
        entering = jnp.where(joined, link_west * (roll(before, 3 + s, 1) - seg[s]), 0.0)
        segout_ref[s] = inflow[s] - flow + jnp.where(lane0, entering, roll(carried, 1, 1))
    copies.append(pltpu.make_async_copy(segout_ref, segout_hbm, sems.at[3]))
    copies[-1].start()
    for copy in copies:
        copy.wait()


HBM = pl.BlockSpec(memory_space=pltpu.HBM)


def call(kernel, outs, *args, in_spec=VMEM, out_spec=VMEM, scratch=()):
    return pl.pallas_call(
        kernel,
        out_shape=[jax.ShapeDtypeStruct(o, F32) if isinstance(o, tuple) else o for o in outs],
        in_specs=[in_spec] * len(args),
        out_specs=[out_spec] * len(outs),
        scratch_shapes=scratch,
        compiler_params=pltpu.CompilerParams(vmem_limit_bytes=16 * 2**20),
    )(*args)


def call_loading(kernel, outs, *args):
    scratch = [pltpu.VMEM(a.shape, a.dtype) for a in args] + [pltpu.SemaphoreType.DMA((len(args),))]
    args = [pltpu.with_memory_space_constraint(a, pltpu.HBM) for a in args]
    return call(kernel, outs, *args, in_spec=HBM, scratch=scratch)


def shift(array, axis, by):
    length = lax.axis_size(axis)
    return lax.ppermute(array, axis, [(i, i + by) for i in range(length) if 0 <= i + by < length])


def body(
    pressure, saturation, old_mass, pore_volume, transmissibility, upwind_code, cell_tangent, segment_pressure,
    segment_tangent, segment_well, link_factor, heel_pressure, perforation_cell, perforation_segment, well_index,
    perforation_count,
):
    p = pressure.reshape(CELL_ROWS, LANES)
    sat = saturation.reshape(2, CELL_ROWS, LANES)
    om = old_mass.reshape(3, CELL_ROWS, LANES)
    pv = pore_volume.reshape(CELL_ROWS, LANES)
    tr = transmissibility.reshape(3, CELL_ROWS, LANES)
    code = upwind_code.reshape(CELL_ROWS, LANES)
    ct = cell_tangent.reshape(2, 3, CELL_ROWS, LANES)

    pay, slots = call_loading(
        slot_kernel, [(TILES * BLOCK, LANES), (16, SLOTS)],
        p, sat, ct, segment_pressure, segment_tangent, perforation_cell, perforation_segment, well_index,
        perforation_count,
    )
    got = lax.all_to_all(pay.reshape(TILES, 1, BLOCK * LANES), "xt", 0, 0, tiled=True)
    got = got.reshape(TILES * BLOCK, LANES)
    xlo, xhi, ylo, yhi, seg = call(
        pack_kernel, [(80, LANES), (96, LANES), (8, LANES), (8, LANES), (48, LANES)],
        p, sat, ct, tr, code, segment_pressure, segment_tangent, segment_well, link_factor, heel_pressure,
    )
    west_xhi = shift(xhi, "xt", 1)
    east_xlo = shift(xlo, "xt", -1)
    north_ylo = shift(ylo, "yt", -1)
    south_yhi = shift(yhi, "yt", 1)
    bal, lane_hot, row_hot, seg_hot = call(
        stencil_kernel,
        [(9, CELL_ROWS, LANES), jax.ShapeDtypeStruct((2 * SLOTS, WIDE), BF16),
         jax.ShapeDtypeStruct((WIDE_ROWS, SLOTS), BF16), jax.ShapeDtypeStruct((4, 2 * LANES, LANES), BF16)],
        p, sat, ct, om, pv, tr, code, slots, xlo, xhi, east_xlo, west_xhi,
    )
    res, prod, seg = call(
        join_kernel, [(3, CELL_ROWS, LANES), (2, 3, CELL_ROWS, LANES), (3, 8, LANES)],
        got, slots, bal, seg, lane_hot, row_hot, seg_hot, ylo, yhi, north_ylo, south_yhi, east_xlo, west_xhi,
        out_spec=HBM,
        scratch=[pltpu.VMEM((9, CELL_ROWS, LANES), F32), pltpu.VMEM((3, 8, LANES), F32), pltpu.SemaphoreType.DMA((4,))],
    )
    return (res.reshape(old_mass.shape), prod.reshape(cell_tangent.shape), seg)


def solution(mesh):
    cell, seg = P(None, "xt", "yt"), P("yt", "xt")
    cell2, cell3, seg2 = P(None, None, "xt", "yt"), P(None, None, None, "xt", "yt"), P(None, "yt", "xt")
    in_specs = (
        cell, cell2, cell2, cell, cell2, cell, cell3, seg, seg2, seg, seg, seg, seg, seg, seg, seg,
    )
    return jax.shard_map(body, mesh=mesh, in_specs=in_specs, out_specs=(cell2, cell3, seg2), check_vma=False)
```

```python
import jax
import jax.numpy as jnp
from jax import lax
from jax.experimental import pallas as pl
from jax.experimental.pallas import tpu as pltpu
from jax.sharding import PartitionSpec as P

COMPRESS = (0.05, 0.1, 0.6)
INV_VISCOSITY = (2.0, 0.5, 5.0)
GRAVITY_HEAD = (0.3, 0.25, 0.05)

NZ = 8
LANES = 128
CELL_ROWS = 64
SLOTS = 512
TILES = 32
PEER = 16
ROWS_A = 24
BLOCK = ROWS_A + 1
WIDE = 256
ORDER = [r // 2 + TILES // 2 * (r % 2) for r in range(TILES)]
PLACE = [ORDER.index(k) for k in range(TILES)]
WIDE_ROWS = 32
F32 = jnp.float32
BF16 = jnp.bfloat16
VMEM = pl.BlockSpec(memory_space=pltpu.VMEM)


def roll(x, shift, axis):
    return pltpu.roll(x, shift % x.shape[axis], axis)


def iota(shape, dim):
    return lax.broadcasted_iota(jnp.int32, shape, dim)


def split(x):
    hi = x.astype(BF16)
    lo = (x - hi.astype(F32)).astype(BF16)
    return hi, lo


def one_hot(mask):
    return jnp.where(mask, 1.0, 0.0).astype(BF16)


def properties(press, water, gas):
    oil = (1.0 - water[0] - gas[0], -water[1] - gas[1], -water[2] - gas[2])
    mobility, mass = [], []
    for phase, sat in enumerate((water, oil, gas)):
        c = COMPRESS[phase]
        base = jnp.exp(c * press[0])
        cb = c * base
        m0 = base * sat[0]
        cs = cb * sat[0]
        m1 = cs * press[1] + base * sat[1]
        m2 = cs * press[2] + base * sat[2]
        v = INV_VISCOSITY[phase]
        vs = v * sat[0]
        vm = v * m0
        mobility.append((m0 * vs, m1 * vs + vm * sat[1], m2 * vs + vm * sat[2]))
        mass.append((m0, m1, m2))
    return mobility, mass


def fluxes(mob_low, mob_up, press_low, press_up, trans, code, direction, heads):
    drop = [trans * (press_low[s] - press_up[s]) for s in range(3)]
    out = []
    for phase in range(3):
        bit = (code & (1 << (3 * direction + phase))) != 0
        up = [jnp.where(bit, mob_up[phase][s], mob_low[phase][s]) for s in range(3)]
        first = drop[0] if heads is None else drop[0] + trans * heads[phase]
        out.append(
            (
                up[0] * first,
                up[1] * first + up[0] * drop[1],
                up[2] * first + up[0] * drop[2],
            )
        )
    return out


def nine(p_ref, s_ref, ct_ref, at):
    return [
        p_ref[at, :], ct_ref[0, 0, at, :], ct_ref[1, 0, at, :],
        s_ref[0, at, :], ct_ref[0, 1, at, :], ct_ref[1, 1, at, :],
        s_ref[1, at, :], ct_ref[0, 2, at, :], ct_ref[1, 2, at, :],
    ]


def exchange(x):
    sub, group = iota((8, LANES), 0), iota((8, LANES), 1) >> 4
    for b in (1, 2, 4):
        s, g = (sub & b) != 0, (group & b) != 0
        down = roll(roll(x, -b, 0), PEER * b, 1)
        up = roll(roll(x, b, 0), -PEER * b, 1)
        x = jnp.where(s == g, x, jnp.where(g, down, up))
    return x


def planes(ref, count):
    return [ref[q * 8:(q + 1) * 8, :] for q in range(count)]


def slot_kernel(p_hbm, s_hbm, ct_hbm, sp_hbm, st_hbm, pc_hbm, ps_hbm, wi_hbm, cnt_hbm, pay_ref, slot_ref,
                p_ref, s_ref, ct_ref, sp_ref, st_ref, pc_ref, ps_ref, wi_ref, cnt_ref, sems):
    pairs = [
        (pc_hbm, pc_ref), (sp_hbm, sp_ref), (st_hbm, st_ref), (cnt_hbm, cnt_ref), (wi_hbm, wi_ref), (ps_hbm, ps_ref),
        (p_hbm, p_ref), (s_hbm, s_ref), (ct_hbm, ct_ref),
    ]
    copies = [pltpu.make_async_copy(src, dst, sems.at[n]) for n, (src, dst) in enumerate(pairs)]
    for copy in copies:
        copy.start()
    owner = iota((TILES, SLOTS), 1) >> 4
    tile_hot = one_hot(iota((TILES, SLOTS), 0) == owner)
    copies[0].wait()
    cell = pc_ref[...]
    lane_hot = one_hot(iota((LANES, SLOTS), 0) == (cell & (LANES - 1)))
    lane_hot = jnp.concatenate([lane_hot, lane_hot], 0)
    row_mask = iota((CELL_ROWS, SLOTS), 0) == (cell >> 7)
    for copy in copies[1:6]:
        copy.wait()
    seg = [sp_ref[...], st_ref[0], st_ref[1]]
    for k in range(TILES):
        for s in range(3):
            pay_ref[pl.ds(k * BLOCK + s * 8, 8), :] = seg[s]
    counts = jnp.broadcast_to(cnt_ref[...].astype(F32).astype(BF16), (8, TILES))
    live = jnp.dot(counts, tile_hot, preferred_element_type=F32)[0:1]
    rank = (iota((1, SLOTS), 1) & (PEER - 1)).astype(F32)
    weight = jnp.where(rank < live, wi_ref[...], 0.0)
    number = ps_ref[...].astype(F32)
    for copy in copies[6:]:
        copy.wait()
    at = pl.ds(0, CELL_ROWS)
    hi, lo = split(jnp.concatenate(nine(p_ref, s_ref, ct_ref, at), 0))
    picked = jnp.dot(jnp.concatenate([hi, lo], 1), lane_hot, preferred_element_type=F32)
    val = [
        jnp.sum(jnp.where(row_mask, picked[q * CELL_ROWS:(q + 1) * CELL_ROWS], 0.0), axis=0, keepdims=True)
        for q in range(9)
    ]
    press = val[0:3]
    mobility, _ = properties(press, val[3:6], val[6:9])
    wl = [[weight * mobility[a][s] for s in range(3)] for a in range(3)]
    total = [wl[0][s] + wl[1][s] + wl[2][s] for s in range(3)]
    carry = [
        total[0] * press[0],
        total[1] * press[0] + total[0] * press[1],
        total[2] * press[0] + total[0] * press[2],
    ]
    sent = jnp.concatenate([number] + carry + total + [jnp.zeros((1, SLOTS), F32)], 0)
    for w in range(4):
        rows = exchange(sent[:, w * LANES:(w + 1) * LANES])
        for k in range(8):
            pay_ref[pl.ds(PLACE[w * 8 + k] * BLOCK + ROWS_A, 1), :] = rows[k:k + 1]
    slot_ref[...] = jnp.concatenate(
        press + [wl[a][s] for s in range(3) for a in range(3)]
        + [cell.astype(F32), number, jnp.zeros((2, SLOTS), F32)], 0
    )


def pack_kernel(p_ref, s_ref, ct_ref, t_ref, code_ref, sp_ref, st_ref, well_ref, link_ref, heel_ref,
                xlo_ref, xhi_ref, ylo_ref, yhi_ref, seg_ref):
    first, last = pl.ds(0, NZ, stride=8), pl.ds(7, NZ, stride=8)
    for q, v in enumerate(nine(p_ref, s_ref, ct_ref, first)):
        xlo_ref[q * 8:(q + 1) * 8, :] = v
    for q, v in enumerate(nine(p_ref, s_ref, ct_ref, last)):
        xhi_ref[q * 8:(q + 1) * 8, :] = v
    xhi_ref[72:80, :] = t_ref[0, last, :]
    xhi_ref[80:88, :] = code_ref[last, :].astype(F32)
    lane = iota((8, LANES), 1)
    seg = [well_ref[...].astype(F32), link_ref[...], sp_ref[...], st_ref[0], st_ref[1], heel_ref[...]]
    for n, v in enumerate(seg):
        seg_ref[n * 8:(n + 1) * 8, :] = v
    left, right = seg[0], seg[0]
    for n in range(1, 5):
        left = jnp.where(lane == n, roll(seg[n], n, 1), left)
        right = jnp.where(lane == LANES - 1 - n, roll(seg[n], -n, 1), right)
    xlo_ref[72:80, :] = left
    xhi_ref[88:96, :] = right
    low = jnp.zeros((8, LANES), F32)
    high = jnp.zeros((8, LANES), F32)
    for z in range(NZ):
        at = pl.ds(z * 8, 8)
        for q, v in enumerate(nine(p_ref, s_ref, ct_ref, at)):
            c = q * 8 + z
            low = jnp.where(lane == c, roll(v, c, 1), low)
            high = jnp.where(lane == c, roll(v, c + 1, 1), high)
        high = jnp.where(lane == 72 + z, roll(t_ref[1, at, :], 73 + z, 1), high)
        high = jnp.where(lane == 80 + z, roll(code_ref[at, :].astype(F32), 81 + z, 1), high)
    ylo_ref[...] = low
    yhi_ref[...] = high


def face(low, up, trans, code, direction):
    return fluxes(
        properties(low[0:3], low[3:6], low[6:9])[0], properties(up[0:3], up[3:6], up[6:9])[0],
        low[0:3], up[0:3], trans, code, direction, None,
    )


def stencil_kernel(p_ref, s_ref, ct_ref, om_ref, pv_ref, t_ref, code_ref, slot_ref, xlo_ref, xhi_ref, exlo_ref, wxhi_ref,
                   bal_ref, lane_hot_ref, row_hot_ref, seg_hot_ref):
    cell = slot_ref[12:13, :].astype(jnp.int32)
    lane_hot = jnp.where(iota((WIDE, SLOTS), 0) == (cell & (WIDE - 1)), 1.0, 0.0).T.astype(BF16)
    lane_hot_ref[0:SLOTS, :] = lane_hot
    lane_hot_ref[SLOTS:2 * SLOTS, :] = lane_hot
    row_hot_ref[...] = one_hot(iota((WIDE_ROWS, SLOTS), 0) == (cell >> 8))
    seg_lane = slot_ref[13:14, :].astype(jnp.int32) & (LANES - 1)
    for w in range(4):
        hot = one_hot(iota((LANES, LANES), 0) == seg_lane[:, w * LANES:(w + 1) * LANES])
        seg_hot_ref[w, 0:LANES, :] = hot
        seg_hot_ref[w, LANES:2 * LANES, :] = hot
    lane = iota((8, LANES), 1)
    sub = iota((8, LANES), 0)
    raw = nine(p_ref, s_ref, ct_ref, pl.ds(0, 8))
    mob, mass = properties(raw[0:3], raw[3:6], raw[6:9])
    press = raw[0:3]
    above = None
    for z in range(NZ):
        at = pl.ds(z * 8, 8)
        code = code_ref[at, :]
        volume = pv_ref[at, :]
        bal = [[volume * mass[a][s] for s in range(3)] for a in range(3)]
        for a in range(3):
            bal[a][0] = bal[a][0] - om_ref[a, at, :]
        for direction, axis, last in ((0, 0, sub == 7), (1, 1, lane == LANES - 1)):
            trans = jnp.where(last, 0.0, t_ref[direction, at, :])
            up_mob = [[roll(mob[a][s], -1, axis) for s in range(3)] for a in range(3)]
            up_press = [roll(press[s], -1, axis) for s in range(3)]
            flux = fluxes(mob, up_mob, press, up_press, trans, code, direction, None)
            for a in range(3):
                for s in range(3):
                    bal[a][s] = bal[a][s] + (flux[a][s] - roll(flux[a][s], 1, axis))
        if above is not None:
            for a in range(3):
                for s in range(3):
                    bal[a][s] = bal[a][s] - above[a][s]
        if z < NZ - 1:
            raw = nine(p_ref, s_ref, ct_ref, pl.ds(z * 8 + 8, 8))
            mob_next, mass = properties(raw[0:3], raw[3:6], raw[6:9])
            above = fluxes(mob, mob_next, press, raw[0:3], t_ref[2, at, :], code, 2, GRAVITY_HEAD)
            for a in range(3):
                for s in range(3):
                    bal[a][s] = bal[a][s] + above[a][s]
            mob, press = mob_next, raw[0:3]
        for a in range(3):
            for s in range(3):
                bal_ref[s * 3 + a, at, :] = bal[a][s]

    top_x = lax.axis_index("xt") == TILES - 1
    own, near = planes(xhi_ref, 11), planes(wxhi_ref, 11)
    east = face(own[0:9], planes(exlo_ref, 9), jnp.where(top_x, 0.0, own[9]), own[10].astype(jnp.int32), 0)
    west = face(near[0:9], planes(xlo_ref, 9), near[9], near[10].astype(jnp.int32), 0)
    first, last = pl.ds(0, NZ, stride=8), pl.ds(7, NZ, stride=8)
    for s in range(3):
        for a in range(3):
            n = s * 3 + a
            bal_ref[n, last, :] = bal_ref[n, last, :] + east[a][s]
            bal_ref[n, first, :] = bal_ref[n, first, :] - west[a][s]


def join_kernel(got_ref, slot_ref, bal_ref, seg_ref, lane_hot_ref, row_hot_ref, seg_hot_ref, ylo_ref, yhi_ref,
                nylo_ref, syhi_ref, exlo_ref, wxhi_ref, res_hbm, prod_hbm, segout_hbm, out_ref, segout_ref, sems):
    top_x = lax.axis_index("xt") == TILES - 1
    top_y = lax.axis_index("yt") == lax.axis_size("yt") - 1
    lane = iota((8, LANES), 1)
    group = iota((1, LANES), 1) >> 4

    half = lane < 64
    own_lo, own_hi, north, south = ylo_ref[...], yhi_ref[...], nylo_ref[...], syhi_ref[...]
    low = [jnp.where(half, roll(own_hi, -8 * q, 1), roll(south, 64 - 8 * q, 1)) for q in range(11)]
    up = [jnp.where(half, roll(north, -8 * q, 1), roll(own_lo, 64 - 8 * q, 1)) for q in range(9)]
    trans = jnp.where(jnp.logical_and(half, top_y), 0.0, low[9])
    rim = face(low[0:9], up, trans, low[10].astype(jnp.int32), 1)
    even = (lane & 1) == 0
    edge = jnp.logical_or(lane == 0, lane == LANES - 1)

    seg_row = slot_ref[13:14, :].astype(jnp.int32) >> 7
    rates = [[] for _ in range(9)]
    for w in range(4):
        cols = slice(w * LANES, (w + 1) * LANES)
        blocks = [got_ref[pl.ds(PLACE[w * 8 + k] * BLOCK, ROWS_A), :] for k in range(8)]
        hi, lo = split(jnp.concatenate(blocks, 0))
        picked = jnp.dot(jnp.concatenate([hi, lo], 1), seg_hot_ref[w], preferred_element_type=F32)
        mine = picked[0:ROWS_A]
        for k in range(1, 8):
            mine = jnp.where(group == k, picked[k * ROWS_A:(k + 1) * ROWS_A], mine)
        row_mask = iota((8, LANES), 0) == seg_row[:, cols]
        at_seg = [
            jnp.sum(jnp.where(row_mask, mine[s * 8:(s + 1) * 8], 0.0), axis=0, keepdims=True) for s in range(3)
        ]
        drop = [slot_ref[s:s + 1, cols] - at_seg[s] for s in range(3)]
        base = [slot_ref[3 + a:4 + a, cols] for a in range(3)]
        for a in range(3):
            rates[a].append(base[a] * drop[0])
            for s in (1, 2):
                r = 3 + s * 3 + a
                rates[s * 3 + a].append(slot_ref[r:r + 1, cols] * drop[0] + base[a] * drop[s])

    row_hot = row_hot_ref[...]
    parts = [split(jnp.concatenate(r, 1)) for r in rates]
    left = jnp.concatenate([jnp.concatenate([row_hot * hi, row_hot * lo], 1) for hi, lo in parts], 0)
    added = jnp.dot(left, lane_hot_ref[...], preferred_element_type=F32)
    copies = []
    for s in range(3):
        for a in range(3):
            n = s * 3 + a
            flux = rim[a][s]
            moved = roll(flux, 65, 1)
            by_parity = (jnp.where(even, flux, -moved), jnp.where(even, -moved, flux))
            for z in range(NZ):
                at = pl.ds(z * 8, 8)
                out_ref[n, at, :] = bal_ref[n, at, :] + jnp.where(
                    edge, roll(by_parity[z % 2], LANES - 1 - z, 1), 0.0
                )
            for h in range(2):
                at = pl.ds(h, WIDE_ROWS, stride=2)
                more = added[n * WIDE_ROWS:(n + 1) * WIDE_ROWS, h * LANES:(h + 1) * LANES]
                out_ref[n, at, :] = out_ref[n, at, :] + more
        copies.append(pltpu.make_async_copy(
            out_ref.at[pl.ds(s * 3, 3)], res_hbm if s == 0 else prod_hbm.at[s - 1], sems.at[s]
        ))
        copies[-1].start()

    told = jnp.concatenate(
        [exchange(got_ref[pl.ds(w * 8 * BLOCK + ROWS_A, 8, stride=BLOCK), :]) for w in range(4)], 1
    )
    number = told[0:1].astype(jnp.int32)
    hot = one_hot(iota((LANES, SLOTS), 0) == (number & (LANES - 1)))
    row_mask = iota((8, SLOTS), 0) == (number >> 7)
    hi, lo = split(jnp.concatenate([jnp.where(row_mask, told[q:q + 1], 0.0) for q in range(1, 7)], 0))
    sums = lax.dot_general(
        jnp.concatenate([hi, lo], 1), jnp.concatenate([hot, hot], 1), (((1,), (1,)), ((), ())),
        preferred_element_type=F32,
    )
    c = [sums[s * 8:(s + 1) * 8] for s in range(3)]
    a = [sums[24 + s * 8:32 + s * 8] for s in range(3)]
    well, link, *seg = planes(seg_ref, 5)
    heel = seg_ref[40:48, :]
    inflow = [
        c[0] - seg[0] * a[0],
        c[1] - seg[0] * a[1] - seg[1] * a[0],
        c[2] - seg[0] * a[2] - seg[2] * a[0],
    ]

    after, before = exlo_ref[72:80, :], wxhi_ref[88:96, :]
    lane0 = lane == 0
    next_well = roll(jnp.where(lane0, after, well), -1, 1)
    linked = jnp.logical_and(next_well == well, jnp.logical_not(jnp.logical_and(top_x, lane == LANES - 1)))
    joined = roll(before, 1, 1) == well
    link_west = roll(before, 2, 1)
    for s in range(3):
        next_press = roll(jnp.where(lane0, roll(after, -2 - s, 1), seg[s]), -1, 1)
        end = heel if s == 0 else jnp.zeros((8, LANES), F32)
        flow = link * (seg[s] - jnp.where(linked, next_press, end))
        carried = jnp.where(linked, flow, 0.0)
        entering = jnp.where(joined, link_west * (roll(before, 3 + s, 1) - seg[s]), 0.0)
        segout_ref[s] = inflow[s] - flow + jnp.where(lane0, entering, roll(carried, 1, 1))
    copies.append(pltpu.make_async_copy(segout_ref, segout_hbm, sems.at[3]))
    copies[-1].start()
    for copy in copies:
        copy.wait()


HBM = pl.BlockSpec(memory_space=pltpu.HBM)


def call(kernel, outs, *args, in_spec=VMEM, out_spec=VMEM, scratch=()):
    return pl.pallas_call(
        kernel,
        out_shape=[jax.ShapeDtypeStruct(o, F32) if isinstance(o, tuple) else o for o in outs],
        in_specs=[in_spec] * len(args),
        out_specs=[out_spec] * len(outs),
        scratch_shapes=scratch,
        compiler_params=pltpu.CompilerParams(vmem_limit_bytes=16 * 2**20),
    )(*args)


def call_loading(kernel, outs, *args):
    scratch = [pltpu.VMEM(a.shape, a.dtype) for a in args] + [pltpu.SemaphoreType.DMA((len(args),))]
    args = [pltpu.with_memory_space_constraint(a, pltpu.HBM) for a in args]
    return call(kernel, outs, *args, in_spec=HBM, scratch=scratch)


def shift(array, axis, by):
    length = lax.axis_size(axis)
    return lax.ppermute(array, axis, [(i, i + by) for i in range(length) if 0 <= i + by < length])


def body(
    pressure, saturation, old_mass, pore_volume, transmissibility, upwind_code, cell_tangent, segment_pressure,
    segment_tangent, segment_well, link_factor, heel_pressure, perforation_cell, perforation_segment, well_index,
    perforation_count,
):
    p = pressure.reshape(CELL_ROWS, LANES)
    sat = saturation.reshape(2, CELL_ROWS, LANES)
    om = old_mass.reshape(3, CELL_ROWS, LANES)
    pv = pore_volume.reshape(CELL_ROWS, LANES)
    tr = transmissibility.reshape(3, CELL_ROWS, LANES)
    code = upwind_code.reshape(CELL_ROWS, LANES)
    ct = cell_tangent.reshape(2, 3, CELL_ROWS, LANES)

    pay, slots = call_loading(
        slot_kernel, [(TILES * BLOCK, LANES), (16, SLOTS)],
        p, sat, ct, segment_pressure, segment_tangent, perforation_cell, perforation_segment, well_index,
        perforation_count,
    )
    got = lax.all_to_all(
        pay.reshape(TILES, 1, BLOCK * LANES), "xt", 0, 0, tiled=True, axis_index_groups=[ORDER]
    )
    got = got.reshape(TILES * BLOCK, LANES)
    xlo, xhi, ylo, yhi, seg = call(
        pack_kernel, [(80, LANES), (96, LANES), (8, LANES), (8, LANES), (48, LANES)],
        p, sat, ct, tr, code, segment_pressure, segment_tangent, segment_well, link_factor, heel_pressure,
    )
    west_xhi = shift(xhi, "xt", 1)
    east_xlo = shift(xlo, "xt", -1)
    north_ylo = shift(ylo, "yt", -1)
    south_yhi = shift(yhi, "yt", 1)
    bal, lane_hot, row_hot, seg_hot = call(
        stencil_kernel,
        [(9, CELL_ROWS, LANES), jax.ShapeDtypeStruct((2 * SLOTS, WIDE), BF16),
         jax.ShapeDtypeStruct((WIDE_ROWS, SLOTS), BF16), jax.ShapeDtypeStruct((4, 2 * LANES, LANES), BF16)],
        p, sat, ct, om, pv, tr, code, slots, xlo, xhi, east_xlo, west_xhi,
    )
    res, prod, seg = call(
        join_kernel, [(3, CELL_ROWS, LANES), (2, 3, CELL_ROWS, LANES), (3, 8, LANES)],
        got, slots, bal, seg, lane_hot, row_hot, seg_hot, ylo, yhi, north_ylo, south_yhi, east_xlo, west_xhi,
        out_spec=HBM,
        scratch=[pltpu.VMEM((9, CELL_ROWS, LANES), F32), pltpu.VMEM((3, 8, LANES), F32), pltpu.SemaphoreType.DMA((4,))],
    )
    return (res.reshape(old_mass.shape), prod.reshape(cell_tangent.shape), seg)


def solution(mesh):
    cell, seg = P(None, "xt", "yt"), P("yt", "xt")
    cell2, cell3, seg2 = P(None, None, "xt", "yt"), P(None, None, None, "xt", "yt"), P(None, "yt", "xt")
    in_specs = (
        cell, cell2, cell2, cell, cell2, cell, cell3, seg, seg2, seg, seg, seg, seg, seg, seg, seg,
    )
    return jax.shard_map(body, mesh=mesh, in_specs=in_specs, out_specs=(cell2, cell3, seg2), check_vma=False)
```

```python
import jax
import jax.numpy as jnp
from jax import lax
from jax.experimental import pallas as pl
from jax.experimental.pallas import tpu as pltpu
from jax.sharding import PartitionSpec as P

COMPRESS = (0.05, 0.1, 0.6)
INV_VISCOSITY = (2.0, 0.5, 5.0)
GRAVITY_HEAD = (0.3, 0.25, 0.05)

NZ = 8
LANES = 128
CELL_ROWS = 64
SLOTS = 512
TILES = 32
PEER = 16
ROWS_A = 24
BLOCK = ROWS_A + 1
WIDE = 256
ORDER = [r // 2 + TILES // 2 * (r % 2) for r in range(TILES)]
PLACE = [ORDER.index(k) for k in range(TILES)]
WIDE_ROWS = 32
F32 = jnp.float32
BF16 = jnp.bfloat16
VMEM = pl.BlockSpec(memory_space=pltpu.VMEM)


def roll(x, shift, axis):
    return pltpu.roll(x, shift % x.shape[axis], axis)


def iota(shape, dim):
    return lax.broadcasted_iota(jnp.int32, shape, dim)


def split(x):
    hi = x.astype(BF16)
    lo = (x - hi.astype(F32)).astype(BF16)
    return hi, lo


def one_hot(mask):
    return jnp.where(mask, 1.0, 0.0).astype(BF16)


def properties(press, water, gas):
    oil = (1.0 - water[0] - gas[0], -water[1] - gas[1], -water[2] - gas[2])
    mobility, mass = [], []
    for phase, sat in enumerate((water, oil, gas)):
        c = COMPRESS[phase]
        base = jnp.exp(c * press[0])
        cb = c * base
        m0 = base * sat[0]
        cs = cb * sat[0]
        m1 = cs * press[1] + base * sat[1]
        m2 = cs * press[2] + base * sat[2]
        v = INV_VISCOSITY[phase]
        vs = v * sat[0]
        vm = v * m0
        mobility.append((m0 * vs, m1 * vs + vm * sat[1], m2 * vs + vm * sat[2]))
        mass.append((m0, m1, m2))
    return mobility, mass


def fluxes(mob_low, mob_up, press_low, press_up, trans, code, direction, heads):
    drop = [trans * (press_low[s] - press_up[s]) for s in range(3)]
    out = []
    for phase in range(3):
        bit = (code & (1 << (3 * direction + phase))) != 0
        up = [jnp.where(bit, mob_up[phase][s], mob_low[phase][s]) for s in range(3)]
        first = drop[0] if heads is None else drop[0] + trans * heads[phase]
        out.append(
            (
                up[0] * first,
                up[1] * first + up[0] * drop[1],
                up[2] * first + up[0] * drop[2],
            )
        )
    return out


def nine(p_ref, s_ref, ct_ref, at):
    return [
        p_ref[at, :], ct_ref[0, 0, at, :], ct_ref[1, 0, at, :],
        s_ref[0, at, :], ct_ref[0, 1, at, :], ct_ref[1, 1, at, :],
        s_ref[1, at, :], ct_ref[0, 2, at, :], ct_ref[1, 2, at, :],
    ]


def exchange(x):
    sub, group = iota((8, LANES), 0), iota((8, LANES), 1) >> 4
    for b in (1, 2, 4):
        s, g = (sub & b) != 0, (group & b) != 0
        down = roll(roll(x, -b, 0), PEER * b, 1)
        up = roll(roll(x, b, 0), -PEER * b, 1)
        x = jnp.where(s == g, x, jnp.where(g, down, up))
    return x


def planes(ref, count):
    return [ref[q * 8:(q + 1) * 8, :] for q in range(count)]


def slot_kernel(p_hbm, s_hbm, ct_hbm, sp_hbm, st_hbm, pc_hbm, ps_hbm, wi_hbm, cnt_hbm, pay_ref, slot_ref,
                p_ref, s_ref, ct_ref, sp_ref, st_ref, pc_ref, ps_ref, wi_ref, cnt_ref, sems):
    pairs = [
        (pc_hbm, pc_ref), (sp_hbm, sp_ref), (st_hbm, st_ref), (cnt_hbm, cnt_ref), (wi_hbm, wi_ref), (ps_hbm, ps_ref),
        (p_hbm, p_ref), (s_hbm, s_ref), (ct_hbm, ct_ref),
    ]
    copies = [pltpu.make_async_copy(src, dst, sems.at[n]) for n, (src, dst) in enumerate(pairs)]
    for copy in copies:
        copy.start()
    owner = iota((TILES, SLOTS), 1) >> 4
    tile_hot = one_hot(iota((TILES, SLOTS), 0) == owner)
    copies[0].wait()
    cell = pc_ref[...]
    lane_hot = one_hot(iota((LANES, SLOTS), 0) == (cell & (LANES - 1)))
    lane_hot = jnp.concatenate([lane_hot, lane_hot], 0)
    row_mask = iota((CELL_ROWS, SLOTS), 0) == (cell >> 7)
    for copy in copies[1:6]:
        copy.wait()
    seg = [sp_ref[...], st_ref[0], st_ref[1]]
    for k in range(TILES):
        for s in range(3):
            pay_ref[pl.ds(k * BLOCK + s * 8, 8), :] = seg[s]
    counts = jnp.broadcast_to(cnt_ref[...].astype(F32).astype(BF16), (8, TILES))
    live = jnp.dot(counts, tile_hot, preferred_element_type=F32)[0:1]
    rank = (iota((1, SLOTS), 1) & (PEER - 1)).astype(F32)
    weight = jnp.where(rank < live, wi_ref[...], 0.0)
    number = ps_ref[...].astype(F32)
    for copy in copies[6:]:
        copy.wait()
    at = pl.ds(0, CELL_ROWS)
    hi, lo = split(jnp.concatenate(nine(p_ref, s_ref, ct_ref, at), 0))
    picked = jnp.dot(jnp.concatenate([hi, lo], 1), lane_hot, preferred_element_type=F32)
    val = [
        jnp.sum(jnp.where(row_mask, picked[q * CELL_ROWS:(q + 1) * CELL_ROWS], 0.0), axis=0, keepdims=True)
        for q in range(9)
    ]
    press = val[0:3]
    mobility, _ = properties(press, val[3:6], val[6:9])
    wl = [[weight * mobility[a][s] for s in range(3)] for a in range(3)]
    total = [wl[0][s] + wl[1][s] + wl[2][s] for s in range(3)]
    carry = [
        total[0] * press[0],
        total[1] * press[0] + total[0] * press[1],
        total[2] * press[0] + total[0] * press[2],
    ]
    sent = jnp.concatenate([number] + carry + total + [jnp.zeros((1, SLOTS), F32)], 0)
    for w in range(4):
        rows = exchange(sent[:, w * LANES:(w + 1) * LANES])
        for k in range(8):
            pay_ref[pl.ds(PLACE[w * 8 + k] * BLOCK + ROWS_A, 1), :] = rows[k:k + 1]
    slot_ref[...] = jnp.concatenate(
        press + [wl[a][s] for s in range(3) for a in range(3)]
        + [cell.astype(F32), number, jnp.zeros((2, SLOTS), F32)], 0
    )


def pack_kernel(p_ref, s_ref, ct_ref, t_ref, code_ref, sp_ref, st_ref, well_ref, link_ref, heel_ref,
                xlo_ref, xhi_ref, ylo_ref, yhi_ref, seg_ref):
    first, last = pl.ds(0, NZ, stride=8), pl.ds(7, NZ, stride=8)
    for q, v in enumerate(nine(p_ref, s_ref, ct_ref, first)):
        xlo_ref[q * 8:(q + 1) * 8, :] = v
    for q, v in enumerate(nine(p_ref, s_ref, ct_ref, last)):
        xhi_ref[q * 8:(q + 1) * 8, :] = v
    xhi_ref[72:80, :] = t_ref[0, last, :]
    xhi_ref[80:88, :] = code_ref[last, :].astype(F32)
    lane = iota((8, LANES), 1)
    seg = [well_ref[...].astype(F32), link_ref[...], sp_ref[...], st_ref[0], st_ref[1], heel_ref[...]]
    for n, v in enumerate(seg):
        seg_ref[n * 8:(n + 1) * 8, :] = v
    left, right = seg[0], seg[0]
    for n in range(1, 5):
        left = jnp.where(lane == n, roll(seg[n], n, 1), left)
        right = jnp.where(lane == LANES - 1 - n, roll(seg[n], -n, 1), right)
    xlo_ref[72:80, :] = left
    xhi_ref[88:96, :] = right
    low = jnp.zeros((8, LANES), F32)
    high = jnp.zeros((8, LANES), F32)
    for z in range(NZ):
        at = pl.ds(z * 8, 8)
        for q, v in enumerate(nine(p_ref, s_ref, ct_ref, at)):
            c = q * 8 + z
            low = jnp.where(lane == c, roll(v, c, 1), low)
            high = jnp.where(lane == c, roll(v, c + 1, 1), high)
        high = jnp.where(lane == 72 + z, roll(t_ref[1, at, :], 73 + z, 1), high)
        high = jnp.where(lane == 80 + z, roll(code_ref[at, :].astype(F32), 81 + z, 1), high)
    ylo_ref[...] = low
    yhi_ref[...] = high


def face(low, up, trans, code, direction):
    return fluxes(
        properties(low[0:3], low[3:6], low[6:9])[0], properties(up[0:3], up[3:6], up[6:9])[0],
        low[0:3], up[0:3], trans, code, direction, None,
    )


def stencil_kernel(p_ref, s_ref, ct_ref, om_ref, pv_ref, t_ref, code_ref, slot_ref, xlo_ref, xhi_ref, exlo_ref, wxhi_ref,
                   bal_ref, lane_hot_ref, row_hot_ref, seg_hot_ref):
    cell = slot_ref[12:13, :].astype(jnp.int32)
    lane_hot = jnp.where(iota((WIDE, SLOTS), 0) == (cell & (WIDE - 1)), 1.0, 0.0).T.astype(BF16)
    lane_hot_ref[0:SLOTS, :] = lane_hot
    lane_hot_ref[SLOTS:2 * SLOTS, :] = lane_hot
    row_hot_ref[...] = one_hot(iota((WIDE_ROWS, SLOTS), 0) == (cell >> 8))
    seg_lane = slot_ref[13:14, :].astype(jnp.int32) & (LANES - 1)
    for w in range(4):
        hot = one_hot(iota((LANES, LANES), 0) == seg_lane[:, w * LANES:(w + 1) * LANES])
        seg_hot_ref[w, 0:LANES, :] = hot
        seg_hot_ref[w, LANES:2 * LANES, :] = hot
    lane = iota((8, LANES), 1)
    sub = iota((8, LANES), 0)
    raw = nine(p_ref, s_ref, ct_ref, pl.ds(0, 8))
    mob, mass = properties(raw[0:3], raw[3:6], raw[6:9])
    press = raw[0:3]
    above = None
    for z in range(NZ):
        at = pl.ds(z * 8, 8)
        code = code_ref[at, :]
        volume = pv_ref[at, :]
        bal = [[volume * mass[a][s] for s in range(3)] for a in range(3)]
        for a in range(3):
            bal[a][0] = bal[a][0] - om_ref[a, at, :]
        for direction, axis, last in ((0, 0, sub == 7), (1, 1, lane == LANES - 1)):
            trans = jnp.where(last, 0.0, t_ref[direction, at, :])
            up_mob = [[roll(mob[a][s], -1, axis) for s in range(3)] for a in range(3)]
            up_press = [roll(press[s], -1, axis) for s in range(3)]
            flux = fluxes(mob, up_mob, press, up_press, trans, code, direction, None)
            for a in range(3):
                for s in range(3):
                    bal[a][s] = bal[a][s] + (flux[a][s] - roll(flux[a][s], 1, axis))
        if above is not None:
            for a in range(3):
                for s in range(3):
                    bal[a][s] = bal[a][s] - above[a][s]
        if z < NZ - 1:
            raw = nine(p_ref, s_ref, ct_ref, pl.ds(z * 8 + 8, 8))
            mob_next, mass = properties(raw[0:3], raw[3:6], raw[6:9])
            above = fluxes(mob, mob_next, press, raw[0:3], t_ref[2, at, :], code, 2, GRAVITY_HEAD)
            for a in range(3):
                for s in range(3):
                    bal[a][s] = bal[a][s] + above[a][s]
            mob, press = mob_next, raw[0:3]
        for a in range(3):
            for s in range(3):
                bal_ref[s * 3 + a, at, :] = bal[a][s]

    top_x = lax.axis_index("xt") == TILES - 1
    own, near = planes(xhi_ref, 11), planes(wxhi_ref, 11)
    east = face(own[0:9], planes(exlo_ref, 9), jnp.where(top_x, 0.0, own[9]), own[10].astype(jnp.int32), 0)
    west = face(near[0:9], planes(xlo_ref, 9), near[9], near[10].astype(jnp.int32), 0)
    first, last = pl.ds(0, NZ, stride=8), pl.ds(7, NZ, stride=8)
    for s in range(3):
        for a in range(3):
            n = s * 3 + a
            bal_ref[n, last, :] = bal_ref[n, last, :] + east[a][s]
            bal_ref[n, first, :] = bal_ref[n, first, :] - west[a][s]


def join_kernel(got_ref, slot_ref, bal_ref, seg_ref, lane_hot_ref, row_hot_ref, seg_hot_ref, ylo_ref, yhi_ref,
                nylo_ref, syhi_ref, exlo_ref, wxhi_ref, res_hbm, prod_hbm, segout_hbm, out_ref, segout_ref, sems):
    top_x = lax.axis_index("xt") == TILES - 1
    top_y = lax.axis_index("yt") == lax.axis_size("yt") - 1
    lane = iota((8, LANES), 1)
    group = iota((1, LANES), 1) >> 4

    half = lane < 64
    own_lo, own_hi, north, south = ylo_ref[...], yhi_ref[...], nylo_ref[...], syhi_ref[...]
    low = [jnp.where(half, roll(own_hi, -8 * q, 1), roll(south, 64 - 8 * q, 1)) for q in range(11)]
    up = [jnp.where(half, roll(north, -8 * q, 1), roll(own_lo, 64 - 8 * q, 1)) for q in range(9)]
    trans = jnp.where(jnp.logical_and(half, top_y), 0.0, low[9])
    rim = face(low[0:9], up, trans, low[10].astype(jnp.int32), 1)
    even = (lane & 1) == 0
    edge = jnp.logical_or(lane == 0, lane == LANES - 1)

    seg_row = slot_ref[13:14, :].astype(jnp.int32) >> 7
    own_tile = iota((8, LANES), 0) == group
    rates = [[] for _ in range(9)]
    for w in range(4):
        cols = slice(w * LANES, (w + 1) * LANES)
        start = PLACE[w * 8] * BLOCK
        blocks = [got_ref[pl.ds(start + r, 8, stride=2 * BLOCK), :] for r in range(ROWS_A)]
        hi, lo = split(jnp.concatenate(blocks, 0))
        picked = jnp.dot(jnp.concatenate([hi, lo], 1), seg_hot_ref[w], preferred_element_type=F32)
        at_seg = []
        for s in range(3):
            mine = picked[s * 64:s * 64 + 8]
            for r in range(1, 8):
                mine = jnp.where(seg_row[:, cols] == r, picked[s * 64 + r * 8:s * 64 + r * 8 + 8], mine)
            at_seg.append(jnp.sum(jnp.where(own_tile, mine, 0.0), axis=0, keepdims=True))
        drop = [slot_ref[s:s + 1, cols] - at_seg[s] for s in range(3)]
        base = [slot_ref[3 + a:4 + a, cols] for a in range(3)]
        for a in range(3):
            rates[a].append(base[a] * drop[0])
            for s in (1, 2):
                r = 3 + s * 3 + a
                rates[s * 3 + a].append(slot_ref[r:r + 1, cols] * drop[0] + base[a] * drop[s])

    row_hot = row_hot_ref[...]
    parts = [split(jnp.concatenate(r, 1)) for r in rates]
    left = jnp.concatenate([jnp.concatenate([row_hot * hi, row_hot * lo], 1) for hi, lo in parts], 0)
    added = jnp.dot(left, lane_hot_ref[...], preferred_element_type=F32)
    copies = []
    for s in range(3):
        for a in range(3):
            n = s * 3 + a
            flux = rim[a][s]
            moved = roll(flux, 65, 1)
            by_parity = (jnp.where(even, flux, -moved), jnp.where(even, -moved, flux))
            for z in range(NZ):
                at = pl.ds(z * 8, 8)
                out_ref[n, at, :] = bal_ref[n, at, :] + jnp.where(
                    edge, roll(by_parity[z % 2], LANES - 1 - z, 1), 0.0
                )
            for h in range(2):
                at = pl.ds(h, WIDE_ROWS, stride=2)
                more = added[n * WIDE_ROWS:(n + 1) * WIDE_ROWS, h * LANES:(h + 1) * LANES]
                out_ref[n, at, :] = out_ref[n, at, :] + more
        copies.append(pltpu.make_async_copy(
            out_ref.at[pl.ds(s * 3, 3)], res_hbm if s == 0 else prod_hbm.at[s - 1], sems.at[s]
        ))
        copies[-1].start()

    told = jnp.concatenate(
        [exchange(got_ref[pl.ds(w * 8 * BLOCK + ROWS_A, 8, stride=BLOCK), :]) for w in range(4)], 1
    )
    number = told[0:1].astype(jnp.int32)
    hot = one_hot(iota((LANES, SLOTS), 0) == (number & (LANES - 1)))
    row_mask = iota((8, SLOTS), 0) == (number >> 7)
    hi, lo = split(jnp.concatenate([jnp.where(row_mask, told[q:q + 1], 0.0) for q in range(1, 7)], 0))
    sums = lax.dot_general(
        jnp.concatenate([hi, lo], 1), jnp.concatenate([hot, hot], 1), (((1,), (1,)), ((), ())),
        preferred_element_type=F32,
    )
    c = [sums[s * 8:(s + 1) * 8] for s in range(3)]
    a = [sums[24 + s * 8:32 + s * 8] for s in range(3)]
    well, link, *seg = planes(seg_ref, 5)
    heel = seg_ref[40:48, :]
    inflow = [
        c[0] - seg[0] * a[0],
        c[1] - seg[0] * a[1] - seg[1] * a[0],
        c[2] - seg[0] * a[2] - seg[2] * a[0],
    ]

    after, before = exlo_ref[72:80, :], wxhi_ref[88:96, :]
    lane0 = lane == 0
    next_well = roll(jnp.where(lane0, after, well), -1, 1)
    linked = jnp.logical_and(next_well == well, jnp.logical_not(jnp.logical_and(top_x, lane == LANES - 1)))
    joined = roll(before, 1, 1) == well
    link_west = roll(before, 2, 1)
    for s in range(3):
        next_press = roll(jnp.where(lane0, roll(after, -2 - s, 1), seg[s]), -1, 1)
        end = heel if s == 0 else jnp.zeros((8, LANES), F32)
        flow = link * (seg[s] - jnp.where(linked, next_press, end))
        carried = jnp.where(linked, flow, 0.0)
        entering = jnp.where(joined, link_west * (roll(before, 3 + s, 1) - seg[s]), 0.0)
        segout_ref[s] = inflow[s] - flow + jnp.where(lane0, entering, roll(carried, 1, 1))
    copies.append(pltpu.make_async_copy(segout_ref, segout_hbm, sems.at[3]))
    copies[-1].start()
    for copy in copies:
        copy.wait()


HBM = pl.BlockSpec(memory_space=pltpu.HBM)


def call(kernel, outs, *args, in_spec=VMEM, out_spec=VMEM, scratch=()):
    return pl.pallas_call(
        kernel,
        out_shape=[jax.ShapeDtypeStruct(o, F32) if isinstance(o, tuple) else o for o in outs],
        in_specs=[in_spec] * len(args),
        out_specs=[out_spec] * len(outs),
        scratch_shapes=scratch,
        compiler_params=pltpu.CompilerParams(vmem_limit_bytes=16 * 2**20),
    )(*args)


def call_loading(kernel, outs, *args):
    scratch = [pltpu.VMEM(a.shape, a.dtype) for a in args] + [pltpu.SemaphoreType.DMA((len(args),))]
    args = [pltpu.with_memory_space_constraint(a, pltpu.HBM) for a in args]
    return call(kernel, outs, *args, in_spec=HBM, scratch=scratch)


def shift(array, axis, by):
    length = lax.axis_size(axis)
    return lax.ppermute(array, axis, [(i, i + by) for i in range(length) if 0 <= i + by < length])


def body(
    pressure, saturation, old_mass, pore_volume, transmissibility, upwind_code, cell_tangent, segment_pressure,
    segment_tangent, segment_well, link_factor, heel_pressure, perforation_cell, perforation_segment, well_index,
    perforation_count,
):
    p = pressure.reshape(CELL_ROWS, LANES)
    sat = saturation.reshape(2, CELL_ROWS, LANES)
    om = old_mass.reshape(3, CELL_ROWS, LANES)
    pv = pore_volume.reshape(CELL_ROWS, LANES)
    tr = transmissibility.reshape(3, CELL_ROWS, LANES)
    code = upwind_code.reshape(CELL_ROWS, LANES)
    ct = cell_tangent.reshape(2, 3, CELL_ROWS, LANES)

    pay, slots = call_loading(
        slot_kernel, [(TILES * BLOCK, LANES), (16, SLOTS)],
        p, sat, ct, segment_pressure, segment_tangent, perforation_cell, perforation_segment, well_index,
        perforation_count,
    )
    got = lax.all_to_all(
        pay.reshape(TILES, 1, BLOCK * LANES), "xt", 0, 0, tiled=True, axis_index_groups=[ORDER]
    )
    got = got.reshape(TILES * BLOCK, LANES)
    xlo, xhi, ylo, yhi, seg = call(
        pack_kernel, [(80, LANES), (96, LANES), (8, LANES), (8, LANES), (48, LANES)],
        p, sat, ct, tr, code, segment_pressure, segment_tangent, segment_well, link_factor, heel_pressure,
    )
    west_xhi = shift(xhi, "xt", 1)
    east_xlo = shift(xlo, "xt", -1)
    north_ylo = shift(ylo, "yt", -1)
    south_yhi = shift(yhi, "yt", 1)
    bal, lane_hot, row_hot, seg_hot = call(
        stencil_kernel,
        [(9, CELL_ROWS, LANES), jax.ShapeDtypeStruct((2 * SLOTS, WIDE), BF16),
         jax.ShapeDtypeStruct((WIDE_ROWS, SLOTS), BF16), jax.ShapeDtypeStruct((4, 2 * LANES, LANES), BF16)],
        p, sat, ct, om, pv, tr, code, slots, xlo, xhi, east_xlo, west_xhi,
    )
    res, prod, seg = call(
        join_kernel, [(3, CELL_ROWS, LANES), (2, 3, CELL_ROWS, LANES), (3, 8, LANES)],
        got, slots, bal, seg, lane_hot, row_hot, seg_hot, ylo, yhi, north_ylo, south_yhi, east_xlo, west_xhi,
        out_spec=HBM,
        scratch=[pltpu.VMEM((9, CELL_ROWS, LANES), F32), pltpu.VMEM((3, 8, LANES), F32), pltpu.SemaphoreType.DMA((4,))],
    )
    return (res.reshape(old_mass.shape), prod.reshape(cell_tangent.shape), seg)


def solution(mesh):
    cell, seg = P(None, "xt", "yt"), P("yt", "xt")
    cell2, cell3, seg2 = P(None, None, "xt", "yt"), P(None, None, None, "xt", "yt"), P(None, "yt", "xt")
    in_specs = (
        cell, cell2, cell2, cell, cell2, cell, cell3, seg, seg2, seg, seg, seg, seg, seg, seg, seg,
    )
    return jax.shard_map(body, mesh=mesh, in_specs=in_specs, out_specs=(cell2, cell3, seg2), check_vma=False)
```

```python
import jax
import jax.numpy as jnp
from jax import lax
from jax.experimental import pallas as pl
from jax.experimental.pallas import tpu as pltpu
from jax.sharding import PartitionSpec as P

COMPRESS = (0.05, 0.1, 0.6)
INV_VISCOSITY = (2.0, 0.5, 5.0)
GRAVITY_HEAD = (0.3, 0.25, 0.05)

NZ = 8
LANES = 128
CELL_ROWS = 64
SLOTS = 512
TILES = 32
PEER = 16
ROWS_A = 24
BLOCK = ROWS_A + 1
WIDE = 256
ORDER = [r // 2 + TILES // 2 * (r % 2) for r in range(TILES)]
PLACE = [ORDER.index(k) for k in range(TILES)]
WIDE_ROWS = 32
F32 = jnp.float32
BF16 = jnp.bfloat16
VMEM = pl.BlockSpec(memory_space=pltpu.VMEM)


def roll(x, shift, axis):
    return pltpu.roll(x, shift % x.shape[axis], axis)


def iota(shape, dim):
    return lax.broadcasted_iota(jnp.int32, shape, dim)


def split(x):
    hi = x.astype(BF16)
    lo = (x - hi.astype(F32)).astype(BF16)
    return hi, lo


def one_hot(mask):
    return jnp.where(mask, 1.0, 0.0).astype(BF16)


def properties(press, water, gas):
    oil = (1.0 - water[0] - gas[0], -water[1] - gas[1], -water[2] - gas[2])
    mobility, mass = [], []
    for phase, sat in enumerate((water, oil, gas)):
        c = COMPRESS[phase]
        base = jnp.exp(c * press[0])
        cb = c * base
        m0 = base * sat[0]
        cs = cb * sat[0]
        m1 = cs * press[1] + base * sat[1]
        m2 = cs * press[2] + base * sat[2]
        v = INV_VISCOSITY[phase]
        vs = v * sat[0]
        vm = v * m0
        mobility.append((m0 * vs, m1 * vs + vm * sat[1], m2 * vs + vm * sat[2]))
        mass.append((m0, m1, m2))
    return mobility, mass


def fluxes(mob_low, mob_up, press_low, press_up, trans, code, direction, heads):
    drop = [trans * (press_low[s] - press_up[s]) for s in range(3)]
    out = []
    for phase in range(3):
        bit = (code & (1 << (3 * direction + phase))) != 0
        up = [jnp.where(bit, mob_up[phase][s], mob_low[phase][s]) for s in range(3)]
        first = drop[0] if heads is None else drop[0] + trans * heads[phase]
        out.append(
            (
                up[0] * first,
                up[1] * first + up[0] * drop[1],
                up[2] * first + up[0] * drop[2],
            )
        )
    return out


def nine(p_ref, s_ref, ct_ref, at):
    return [
        p_ref[at, :], ct_ref[0, 0, at, :], ct_ref[1, 0, at, :],
        s_ref[0, at, :], ct_ref[0, 1, at, :], ct_ref[1, 1, at, :],
        s_ref[1, at, :], ct_ref[0, 2, at, :], ct_ref[1, 2, at, :],
    ]


def exchange(x):
    sub, group = iota((8, LANES), 0), iota((8, LANES), 1) >> 4
    for b in (1, 2, 4):
        s, g = (sub & b) != 0, (group & b) != 0
        down = roll(roll(x, -b, 0), PEER * b, 1)
        up = roll(roll(x, b, 0), -PEER * b, 1)
        x = jnp.where(s == g, x, jnp.where(g, down, up))
    return x


def planes(ref, count):
    return [ref[q * 8:(q + 1) * 8, :] for q in range(count)]


def slot_kernel(p_hbm, s_hbm, ct_hbm, sp_hbm, st_hbm, pc_hbm, ps_hbm, wi_hbm, cnt_hbm, pay_ref, slot_ref,
                p_ref, s_ref, ct_ref, sp_ref, st_ref, pc_ref, ps_ref, wi_ref, cnt_ref, sems):
    pairs = [
        (pc_hbm, pc_ref), (sp_hbm, sp_ref), (st_hbm, st_ref), (cnt_hbm, cnt_ref), (wi_hbm, wi_ref), (ps_hbm, ps_ref),
        (p_hbm, p_ref), (s_hbm, s_ref), (ct_hbm, ct_ref),
    ]
    copies = [pltpu.make_async_copy(src, dst, sems.at[n]) for n, (src, dst) in enumerate(pairs)]
    for copy in copies:
        copy.start()
    owner = iota((TILES, SLOTS), 1) >> 4
    tile_hot = one_hot(iota((TILES, SLOTS), 0) == owner)
    copies[0].wait()
    cell = pc_ref[...]
    lane_hot = one_hot(iota((WIDE, SLOTS), 0) == (cell & (WIDE - 1)))
    lane_hot = jnp.concatenate([lane_hot, lane_hot], 0)
    row_mask = iota((WIDE_ROWS, SLOTS), 0) == (cell >> 8)
    for copy in copies[1:6]:
        copy.wait()
    seg = [sp_ref[...], st_ref[0], st_ref[1]]
    for k in range(TILES):
        for s in range(3):
            pay_ref[pl.ds(k * BLOCK + s * 8, 8), :] = seg[s]
    counts = jnp.broadcast_to(cnt_ref[...].astype(F32).astype(BF16), (8, TILES))
    live = jnp.dot(counts, tile_hot, preferred_element_type=F32)[0:1]
    rank = (iota((1, SLOTS), 1) & (PEER - 1)).astype(F32)
    weight = jnp.where(rank < live, wi_ref[...], 0.0)
    number = ps_ref[...].astype(F32)
    for copy in copies[6:]:
        copy.wait()
    halves = [nine(p_ref, s_ref, ct_ref, pl.ds(h, WIDE_ROWS, stride=2)) for h in range(2)]
    hi, lo = split(jnp.concatenate([jnp.concatenate(half, 0) for half in halves], 1))
    picked = jnp.dot(jnp.concatenate([hi, lo], 1), lane_hot, preferred_element_type=F32)
    val = [
        jnp.sum(jnp.where(row_mask, picked[q * WIDE_ROWS:(q + 1) * WIDE_ROWS], 0.0), axis=0, keepdims=True)
        for q in range(9)
    ]
    press = val[0:3]
    mobility, _ = properties(press, val[3:6], val[6:9])
    wl = [[weight * mobility[a][s] for s in range(3)] for a in range(3)]
    total = [wl[0][s] + wl[1][s] + wl[2][s] for s in range(3)]
    carry = [
        total[0] * press[0],
        total[1] * press[0] + total[0] * press[1],
        total[2] * press[0] + total[0] * press[2],
    ]
    sent = jnp.concatenate([number] + carry + total + [jnp.zeros((1, SLOTS), F32)], 0)
    for w in range(4):
        rows = exchange(sent[:, w * LANES:(w + 1) * LANES])
        for k in range(8):
            pay_ref[pl.ds(PLACE[w * 8 + k] * BLOCK + ROWS_A, 1), :] = rows[k:k + 1]
    slot_ref[...] = jnp.concatenate(
        press + [wl[a][s] for s in range(3) for a in range(3)]
        + [cell.astype(F32), number, jnp.zeros((2, SLOTS), F32)], 0
    )


def pack_kernel(p_ref, s_ref, ct_ref, t_ref, code_ref, sp_ref, st_ref, well_ref, link_ref, heel_ref,
                xlo_ref, xhi_ref, ylo_ref, yhi_ref, seg_ref):
    first, last = pl.ds(0, NZ, stride=8), pl.ds(7, NZ, stride=8)
    for q, v in enumerate(nine(p_ref, s_ref, ct_ref, first)):
        xlo_ref[q * 8:(q + 1) * 8, :] = v
    for q, v in enumerate(nine(p_ref, s_ref, ct_ref, last)):
        xhi_ref[q * 8:(q + 1) * 8, :] = v
    xhi_ref[72:80, :] = t_ref[0, last, :]
    xhi_ref[80:88, :] = code_ref[last, :].astype(F32)
    lane = iota((8, LANES), 1)
    seg = [well_ref[...].astype(F32), link_ref[...], sp_ref[...], st_ref[0], st_ref[1], heel_ref[...]]
    for n, v in enumerate(seg):
        seg_ref[n * 8:(n + 1) * 8, :] = v
    left, right = seg[0], seg[0]
    for n in range(1, 5):
        left = jnp.where(lane == n, roll(seg[n], n, 1), left)
        right = jnp.where(lane == LANES - 1 - n, roll(seg[n], -n, 1), right)
    xlo_ref[72:80, :] = left
    xhi_ref[88:96, :] = right
    low = jnp.zeros((8, LANES), F32)
    high = jnp.zeros((8, LANES), F32)
    for z in range(NZ):
        at = pl.ds(z * 8, 8)
        for q, v in enumerate(nine(p_ref, s_ref, ct_ref, at)):
            c = q * 8 + z
            low = jnp.where(lane == c, roll(v, c, 1), low)
            high = jnp.where(lane == c, roll(v, c + 1, 1), high)
        high = jnp.where(lane == 72 + z, roll(t_ref[1, at, :], 73 + z, 1), high)
        high = jnp.where(lane == 80 + z, roll(code_ref[at, :].astype(F32), 81 + z, 1), high)
    ylo_ref[...] = low
    yhi_ref[...] = high


def face(low, up, trans, code, direction):
    return fluxes(
        properties(low[0:3], low[3:6], low[6:9])[0], properties(up[0:3], up[3:6], up[6:9])[0],
        low[0:3], up[0:3], trans, code, direction, None,
    )


def stencil_kernel(p_ref, s_ref, ct_ref, om_ref, pv_ref, t_ref, code_ref, slot_ref, xlo_ref, xhi_ref, exlo_ref, wxhi_ref,
                   bal_ref, lane_hot_ref, row_hot_ref, seg_hot_ref):
    cell = slot_ref[12:13, :].astype(jnp.int32)
    lane_hot = jnp.where(iota((WIDE, SLOTS), 0) == (cell & (WIDE - 1)), 1.0, 0.0).T.astype(BF16)
    lane_hot_ref[0:SLOTS, :] = lane_hot
    lane_hot_ref[SLOTS:2 * SLOTS, :] = lane_hot
    row_hot_ref[...] = one_hot(iota((WIDE_ROWS, SLOTS), 0) == (cell >> 8))
    seg_lane = slot_ref[13:14, :].astype(jnp.int32) & (LANES - 1)
    for w in range(4):
        hot = one_hot(iota((LANES, LANES), 0) == seg_lane[:, w * LANES:(w + 1) * LANES])
        seg_hot_ref[w, 0:LANES, :] = hot
        seg_hot_ref[w, LANES:2 * LANES, :] = hot
    lane = iota((8, LANES), 1)
    sub = iota((8, LANES), 0)
    raw = nine(p_ref, s_ref, ct_ref, pl.ds(0, 8))
    mob, mass = properties(raw[0:3], raw[3:6], raw[6:9])
    press = raw[0:3]
    above = None
    for z in range(NZ):
        at = pl.ds(z * 8, 8)
        code = code_ref[at, :]
        volume = pv_ref[at, :]
        bal = [[volume * mass[a][s] for s in range(3)] for a in range(3)]
        for a in range(3):
            bal[a][0] = bal[a][0] - om_ref[a, at, :]
        for direction, axis, last in ((0, 0, sub == 7), (1, 1, lane == LANES - 1)):
            trans = jnp.where(last, 0.0, t_ref[direction, at, :])
            up_mob = [[roll(mob[a][s], -1, axis) for s in range(3)] for a in range(3)]
            up_press = [roll(press[s], -1, axis) for s in range(3)]
            flux = fluxes(mob, up_mob, press, up_press, trans, code, direction, None)
            for a in range(3):
                for s in range(3):
                    bal[a][s] = bal[a][s] + (flux[a][s] - roll(flux[a][s], 1, axis))
        if above is not None:
            for a in range(3):
                for s in range(3):
                    bal[a][s] = bal[a][s] - above[a][s]
        if z < NZ - 1:
            raw = nine(p_ref, s_ref, ct_ref, pl.ds(z * 8 + 8, 8))
            mob_next, mass = properties(raw[0:3], raw[3:6], raw[6:9])
            above = fluxes(mob, mob_next, press, raw[0:3], t_ref[2, at, :], code, 2, GRAVITY_HEAD)
            for a in range(3):
                for s in range(3):
                    bal[a][s] = bal[a][s] + above[a][s]
            mob, press = mob_next, raw[0:3]
        for a in range(3):
            for s in range(3):
                bal_ref[s * 3 + a, at, :] = bal[a][s]

    top_x = lax.axis_index("xt") == TILES - 1
    own, near = planes(xhi_ref, 11), planes(wxhi_ref, 11)
    east = face(own[0:9], planes(exlo_ref, 9), jnp.where(top_x, 0.0, own[9]), own[10].astype(jnp.int32), 0)
    west = face(near[0:9], planes(xlo_ref, 9), near[9], near[10].astype(jnp.int32), 0)
    first, last = pl.ds(0, NZ, stride=8), pl.ds(7, NZ, stride=8)
    for s in range(3):
        for a in range(3):
            n = s * 3 + a
            bal_ref[n, last, :] = bal_ref[n, last, :] + east[a][s]
            bal_ref[n, first, :] = bal_ref[n, first, :] - west[a][s]


def join_kernel(got_ref, slot_ref, bal_ref, seg_ref, lane_hot_ref, row_hot_ref, seg_hot_ref, ylo_ref, yhi_ref,
                nylo_ref, syhi_ref, exlo_ref, wxhi_ref, res_hbm, prod_hbm, segout_hbm, out_ref, segout_ref, sems):
    top_x = lax.axis_index("xt") == TILES - 1
    top_y = lax.axis_index("yt") == lax.axis_size("yt") - 1
    lane = iota((8, LANES), 1)
    group = iota((1, LANES), 1) >> 4

    half = lane < 64
    own_lo, own_hi, north, south = ylo_ref[...], yhi_ref[...], nylo_ref[...], syhi_ref[...]
    low = [jnp.where(half, roll(own_hi, -8 * q, 1), roll(south, 64 - 8 * q, 1)) for q in range(11)]
    up = [jnp.where(half, roll(north, -8 * q, 1), roll(own_lo, 64 - 8 * q, 1)) for q in range(9)]
    trans = jnp.where(jnp.logical_and(half, top_y), 0.0, low[9])
    rim = face(low[0:9], up, trans, low[10].astype(jnp.int32), 1)
    even = (lane & 1) == 0
    edge = jnp.logical_or(lane == 0, lane == LANES - 1)

    seg_row = slot_ref[13:14, :].astype(jnp.int32) >> 7
    own_tile = iota((8, LANES), 0) == group
    rates = [[] for _ in range(9)]
    for w in range(4):
        cols = slice(w * LANES, (w + 1) * LANES)
        start = PLACE[w * 8] * BLOCK
        blocks = [got_ref[pl.ds(start + r, 8, stride=2 * BLOCK), :] for r in range(ROWS_A)]
        hi, lo = split(jnp.concatenate(blocks, 0))
        picked = jnp.dot(jnp.concatenate([hi, lo], 1), seg_hot_ref[w], preferred_element_type=F32)
        at_seg = []
        for s in range(3):
            mine = picked[s * 64:s * 64 + 8]
            for r in range(1, 8):
                mine = jnp.where(seg_row[:, cols] == r, picked[s * 64 + r * 8:s * 64 + r * 8 + 8], mine)
            at_seg.append(jnp.sum(jnp.where(own_tile, mine, 0.0), axis=0, keepdims=True))
        drop = [slot_ref[s:s + 1, cols] - at_seg[s] for s in range(3)]
        base = [slot_ref[3 + a:4 + a, cols] for a in range(3)]
        for a in range(3):
            rates[a].append(base[a] * drop[0])
            for s in (1, 2):
                r = 3 + s * 3 + a
                rates[s * 3 + a].append(slot_ref[r:r + 1, cols] * drop[0] + base[a] * drop[s])

    row_hot = row_hot_ref[...]
    parts = [split(jnp.concatenate(r, 1)) for r in rates]
    left = jnp.concatenate([jnp.concatenate([row_hot * hi, row_hot * lo], 1) for hi, lo in parts], 0)
    added = jnp.dot(left, lane_hot_ref[...], preferred_element_type=F32)
    copies = []
    for s in range(3):
        for a in range(3):
            n = s * 3 + a
            flux = rim[a][s]
            moved = roll(flux, 65, 1)
            by_parity = (jnp.where(even, flux, -moved), jnp.where(even, -moved, flux))
            for z in range(NZ):
                at = pl.ds(z * 8, 8)
                out_ref[n, at, :] = bal_ref[n, at, :] + jnp.where(
                    edge, roll(by_parity[z % 2], LANES - 1 - z, 1), 0.0
                )
            for h in range(2):
                at = pl.ds(h, WIDE_ROWS, stride=2)
                more = added[n * WIDE_ROWS:(n + 1) * WIDE_ROWS, h * LANES:(h + 1) * LANES]
                out_ref[n, at, :] = out_ref[n, at, :] + more
        copies.append(pltpu.make_async_copy(
            out_ref.at[pl.ds(s * 3, 3)], res_hbm if s == 0 else prod_hbm.at[s - 1], sems.at[s]
        ))
        copies[-1].start()

    told = jnp.concatenate(
        [exchange(got_ref[pl.ds(w * 8 * BLOCK + ROWS_A, 8, stride=BLOCK), :]) for w in range(4)], 1
    )
    number = told[0:1].astype(jnp.int32)
    hot = one_hot(iota((LANES, SLOTS), 0) == (number & (LANES - 1)))
    row_mask = iota((8, SLOTS), 0) == (number >> 7)
    hi, lo = split(jnp.concatenate([jnp.where(row_mask, told[q:q + 1], 0.0) for q in range(1, 7)], 0))
    sums = lax.dot_general(
        jnp.concatenate([hi, lo], 1), jnp.concatenate([hot, hot], 1), (((1,), (1,)), ((), ())),
        preferred_element_type=F32,
    )
    c = [sums[s * 8:(s + 1) * 8] for s in range(3)]
    a = [sums[24 + s * 8:32 + s * 8] for s in range(3)]
    well, link, *seg = planes(seg_ref, 5)
    heel = seg_ref[40:48, :]
    inflow = [
        c[0] - seg[0] * a[0],
        c[1] - seg[0] * a[1] - seg[1] * a[0],
        c[2] - seg[0] * a[2] - seg[2] * a[0],
    ]

    after, before = exlo_ref[72:80, :], wxhi_ref[88:96, :]
    lane0 = lane == 0
    next_well = roll(jnp.where(lane0, after, well), -1, 1)
    linked = jnp.logical_and(next_well == well, jnp.logical_not(jnp.logical_and(top_x, lane == LANES - 1)))
    joined = roll(before, 1, 1) == well
    link_west = roll(before, 2, 1)
    for s in range(3):
        next_press = roll(jnp.where(lane0, roll(after, -2 - s, 1), seg[s]), -1, 1)
        end = heel if s == 0 else jnp.zeros((8, LANES), F32)
        flow = link * (seg[s] - jnp.where(linked, next_press, end))
        carried = jnp.where(linked, flow, 0.0)
        entering = jnp.where(joined, link_west * (roll(before, 3 + s, 1) - seg[s]), 0.0)
        segout_ref[s] = inflow[s] - flow + jnp.where(lane0, entering, roll(carried, 1, 1))
    copies.append(pltpu.make_async_copy(segout_ref, segout_hbm, sems.at[3]))
    copies[-1].start()
    for copy in copies:
        copy.wait()


HBM = pl.BlockSpec(memory_space=pltpu.HBM)


def call(kernel, outs, *args, in_spec=VMEM, out_spec=VMEM, scratch=()):
    return pl.pallas_call(
        kernel,
        out_shape=[jax.ShapeDtypeStruct(o, F32) if isinstance(o, tuple) else o for o in outs],
        in_specs=[in_spec] * len(args),
        out_specs=[out_spec] * len(outs),
        scratch_shapes=scratch,
        compiler_params=pltpu.CompilerParams(vmem_limit_bytes=16 * 2**20),
    )(*args)


def call_loading(kernel, outs, *args):
    scratch = [pltpu.VMEM(a.shape, a.dtype) for a in args] + [pltpu.SemaphoreType.DMA((len(args),))]
    args = [pltpu.with_memory_space_constraint(a, pltpu.HBM) for a in args]
    return call(kernel, outs, *args, in_spec=HBM, scratch=scratch)


def shift(array, axis, by):
    length = lax.axis_size(axis)
    return lax.ppermute(array, axis, [(i, i + by) for i in range(length) if 0 <= i + by < length])


def body(
    pressure, saturation, old_mass, pore_volume, transmissibility, upwind_code, cell_tangent, segment_pressure,
    segment_tangent, segment_well, link_factor, heel_pressure, perforation_cell, perforation_segment, well_index,
    perforation_count,
):
    p = pressure.reshape(CELL_ROWS, LANES)
    sat = saturation.reshape(2, CELL_ROWS, LANES)
    om = old_mass.reshape(3, CELL_ROWS, LANES)
    pv = pore_volume.reshape(CELL_ROWS, LANES)
    tr = transmissibility.reshape(3, CELL_ROWS, LANES)
    code = upwind_code.reshape(CELL_ROWS, LANES)
    ct = cell_tangent.reshape(2, 3, CELL_ROWS, LANES)

    pay, slots = call_loading(
        slot_kernel, [(TILES * BLOCK, LANES), (16, SLOTS)],
        p, sat, ct, segment_pressure, segment_tangent, perforation_cell, perforation_segment, well_index,
        perforation_count,
    )
    got = lax.all_to_all(
        pay.reshape(TILES, 1, BLOCK * LANES), "xt", 0, 0, tiled=True, axis_index_groups=[ORDER]
    )
    got = got.reshape(TILES * BLOCK, LANES)
    xlo, xhi, ylo, yhi, seg = call(
        pack_kernel, [(80, LANES), (96, LANES), (8, LANES), (8, LANES), (48, LANES)],
        p, sat, ct, tr, code, segment_pressure, segment_tangent, segment_well, link_factor, heel_pressure,
    )
    west_xhi = shift(xhi, "xt", 1)
    east_xlo = shift(xlo, "xt", -1)
    north_ylo = shift(ylo, "yt", -1)
    south_yhi = shift(yhi, "yt", 1)
    bal, lane_hot, row_hot, seg_hot = call(
        stencil_kernel,
        [(9, CELL_ROWS, LANES), jax.ShapeDtypeStruct((2 * SLOTS, WIDE), BF16),
         jax.ShapeDtypeStruct((WIDE_ROWS, SLOTS), BF16), jax.ShapeDtypeStruct((4, 2 * LANES, LANES), BF16)],
        p, sat, ct, om, pv, tr, code, slots, xlo, xhi, east_xlo, west_xhi,
    )
    res, prod, seg = call(
        join_kernel, [(3, CELL_ROWS, LANES), (2, 3, CELL_ROWS, LANES), (3, 8, LANES)],
        got, slots, bal, seg, lane_hot, row_hot, seg_hot, ylo, yhi, north_ylo, south_yhi, east_xlo, west_xhi,
        out_spec=HBM,
        scratch=[pltpu.VMEM((9, CELL_ROWS, LANES), F32), pltpu.VMEM((3, 8, LANES), F32), pltpu.SemaphoreType.DMA((4,))],
    )
    return (res.reshape(old_mass.shape), prod.reshape(cell_tangent.shape), seg)


def solution(mesh):
    cell, seg = P(None, "xt", "yt"), P("yt", "xt")
    cell2, cell3, seg2 = P(None, None, "xt", "yt"), P(None, None, None, "xt", "yt"), P(None, "yt", "xt")
    in_specs = (
        cell, cell2, cell2, cell, cell2, cell, cell3, seg, seg2, seg, seg, seg, seg, seg, seg, seg,
    )
    return jax.shard_map(body, mesh=mesh, in_specs=in_specs, out_specs=(cell2, cell3, seg2), check_vma=False)
```
